512 devices in a mesh: ctx: 32 (over x, z), exp: 16 (over y, core).
Axes of the slice: x: 4, y: 8, z: 8, core: 2. Of those that a mesh axis runs over, the one named last changes fastest.
Arguments:
- q_spikes: bfloat16 [16384, 4096], P('ctx', 'exp'), may hold values from -1 to 1, as said below
- k_spikes: bfloat16 [16384, 4096], P('ctx', 'exp'), may hold values from -1 to 1, as said below
- v_spikes: bfloat16 [16384, 4096], P('ctx', 'exp'), may hold values from -1 to 1, as said below
- log_decay: float32 [16384, 32], P('ctx', 'exp'), may hold values from -1 to 0, as said below
- norm_gain: float32 [4096], P('exp'), may hold values from 0.1 to 1.9
- out_weight: bfloat16 [4096, 4096], P('exp'), may hold values from -0.09375 to 0.09375
- residual: bfloat16 [16384, 4096], P(('ctx', 'exp')), may hold values from -6 to 6
Outputs:
- mixed: bfloat16 [16384, 4096], P(('ctx', 'exp'))
The draws below stay inside these ranges and needn't reach their ends.
Inputs may be any that keep to these rules, and one draw needn't show every extreme that they name: `q_spikes`: every entry is -1, 0 or 1. `k_spikes`: every entry is -1, 0 or 1. `v_spikes`: every entry is -1, 0 or 1. `log_decay`: every entry is negative.
All inputs are finite; a program needn't handle non-finite values.
Results may differ from the reference program's by a relative error of at most 0.015.
Values may be sent and summed in bfloat16 or wider, within the bound.
A program may use at most 64 MiB of HBM per device.

```python
import jax
import jax.numpy as jnp
from jax import lax

D = 4096
FOCUS_CHANNELS = 32
HD = 128
TOK_DEV = 512
TIMELINE_SPAN = 16384
N_EXP = 16


def spike_table(key):
    levels = jax.random.randint(key, (TIMELINE_SPAN, FOCUS_CHANNELS * HD), 0, 4)
    plus = levels == 0
    minus = levels == 1
    return jnp.where(plus, 1.0, 0.0).astype(jnp.float32) - jnp.where(minus, 1.0, 0.0).astype(jnp.float32)


def draw_q_spikes(key, part):
    return spike_table(jax.random.fold_in(key, 11)).astype(jnp.bfloat16)


def draw_k_spikes(key, part):
    return spike_table(jax.random.fold_in(key, 23)).astype(jnp.bfloat16)


def draw_v_spikes(key, part):
    return spike_table(jax.random.fold_in(key, 37)).astype(jnp.bfloat16)


def draw_log_decay(key, part):
    table_entries_to_fetch = jax.random.split(jax.random.fold_in(key, 51), 6)
    fast_share = 0.5
    fast = jax.random.uniform(table_entries_to_fetch[0], (FOCUS_CHANNELS,)) < fast_share
    fast_rate = jnp.exp(jax.random.uniform(table_entries_to_fetch[1], (FOCUS_CHANNELS,), jnp.float32, jnp.log(1.0 / 50.0), jnp.log(1.0 / 30.0)))
    slow_rate = jax.random.uniform(table_entries_to_fetch[2], (FOCUS_CHANNELS,), jnp.float32, 0.2, 1.0) / TIMELINE_SPAN
    baseline_voltage = jnp.where(fast, fast_rate, slow_rate)
    perturbation_displacement = jnp.exp(jax.random.uniform(table_entries_to_fetch[3], (TIMELINE_SPAN, FOCUS_CHANNELS), jnp.float32, jnp.log(0.5), jnp.log(2.0)))
    emission_sequence = jax.random.uniform(table_entries_to_fetch[4], (TIMELINE_SPAN, FOCUS_CHANNELS)) < 2.5 / TIMELINE_SPAN
    emission_cutoff = jnp.log(jax.random.uniform(table_entries_to_fetch[5], (TIMELINE_SPAN, FOCUS_CHANNELS), jnp.float32, 0.5, 0.8))
    return -baseline_voltage[None, :] * perturbation_displacement + jnp.where(emission_sequence, emission_cutoff, 0.0)


def level_of(rng, shape, shards, least, top_value):
    def one(position, blocks):
        draws = jax.random.uniform(jax.random.fold_in(jax.random.fold_in(rng, 6), position), (blocks,), jnp.float32, least / len(shards), top_value / len(shards))
        return jnp.repeat(jnp.exp(draws), shape[position] // blocks).reshape((-1,) + (1,) * (len(shape) - position - 1))

    loudness = one(*shards[0])
    for cut in shards[1:]:
        loudness = loudness * one(*cut)
    return loudness


def gaussian(own_key, shape, scale, reach, cuts=(), held_as=jnp.bfloat16):
    entries = scale * jax.random.normal(own_key, shape, jnp.float32)
    if cuts:
        entries = entries * level_of(own_key, shape, cuts, -0.22, 0.18)
    return jnp.clip(entries, -reach, reach).astype(held_as)


def setup_inputs(seed: int = 0) -> dict:
    splits = jax.random.split(jax.random.key(seed), 8)
    q_spikes = draw_q_spikes(jax.random.fold_in(splits[7], 71), 0)
    k_spikes = draw_k_spikes(jax.random.fold_in(splits[7], 71), 0)
    v_spikes = draw_v_spikes(jax.random.fold_in(splits[7], 71), 0)
    log_decay = draw_log_decay(jax.random.fold_in(splits[7], 71), 0)
    norm_gain = jnp.clip(1.0 + 0.18 * jax.random.normal(splits[4], (FOCUS_CHANNELS * HD,), jnp.float32), 0.1, 1.9)
    out_weight = gaussian(splits[5], (FOCUS_CHANNELS * HD, D), (FOCUS_CHANNELS * HD) ** -0.5, 0.09375, ((0, 16),))
    residual = gaussian(splits[6], (TIMELINE_SPAN, D), 1.0, 6.0, ((0, 512),))
    return dict(q_spikes=q_spikes, k_spikes=k_spikes, v_spikes=v_spikes, log_decay=log_decay, norm_gain=norm_gain, out_weight=out_weight, residual=residual)


HIGH = lax.Precision.HIGHEST

def block_step(state, inputs):
    query, key, value, logd = inputs
    cum = jnp.cumsum(logd, axis=0)
    count = query.shape[0]
    place = jnp.arange(count)
    causal = place[:, None] >= place[None, :]
    spread = cum[:, None, :] - cum[None, :, :]
    weight = jnp.exp(jnp.where(causal[:, :, None], spread, -jnp.inf))
    scores = jnp.einsum('thd,shd->tsh', query, key, precision=HIGH) * weight
    local = jnp.einsum('tsh,she->the', scores, value, precision=HIGH)
    carried = jnp.einsum('thd,hde->the', query, state, precision=HIGH) * jnp.exp(cum)[:, :, None]
    total = cum[-1]
    keyed = key * jnp.exp(total[None, :] - cum)[:, :, None]
    fresh = state * jnp.exp(total)[:, None, None] + jnp.einsum('shd,she->hde', keyed, value, precision=HIGH)
    return (fresh, local + carried)

def reference(q_spikes, k_spikes, v_spikes, log_decay, norm_gain, out_weight, residual):
    blocks = TIMELINE_SPAN // TOK_DEV
    query = q_spikes.astype(jnp.float32).reshape(blocks, TOK_DEV, FOCUS_CHANNELS, HD)
    key = k_spikes.astype(jnp.float32).reshape(blocks, TOK_DEV, FOCUS_CHANNELS, HD)
    value = v_spikes.astype(jnp.float32).reshape(blocks, TOK_DEV, FOCUS_CHANNELS, HD)
    logd = log_decay.reshape(blocks, TOK_DEV, FOCUS_CHANNELS)
    start = jnp.zeros((FOCUS_CHANNELS, HD, HD), jnp.float32)
    final, attended = lax.scan(block_step, start, (query, key, value, logd))
    attended = attended.reshape(TIMELINE_SPAN, FOCUS_CHANNELS, HD)
    scale = jnp.sqrt(lax.optimization_barrier(jnp.mean(attended * attended, axis=-1, keepdims=True)) + 1e-06)
    normed = (attended / scale * norm_gain.reshape(FOCUS_CHANNELS, HD)).astype(jnp.bfloat16).reshape(TIMELINE_SPAN, FOCUS_CHANNELS * HD)
    cols = FOCUS_CHANNELS * HD // N_EXP
    summed = jnp.zeros((TIMELINE_SPAN, D), jnp.float32)
    for group in range(N_EXP):
        partial_value = jnp.dot(normed[:, group * cols:(group + 1) * cols], out_weight[group * cols:(group + 1) * cols], preferred_element_type=jnp.float32).astype(jnp.bfloat16)
        partial_value = lax.optimization_barrier(partial_value)
        summed = summed + partial_value.astype(jnp.float32)
    return (summed + residual.astype(jnp.float32)).astype(jnp.bfloat16)
```

```python
import functools

import jax
import jax.numpy as jnp
from jax import lax
from jax.experimental import pallas as pl
from jax.experimental.pallas import tpu as pltpu
from jax.sharding import PartitionSpec as P

MESH = pl.DeviceIdType.MESH
F32, BF16 = jnp.float32, jnp.bfloat16
NZ = 8
HEADS, HD = 2, 128
SLICE = HD // NZ
BODY = HEADS * SLICE
MSG = BODY + 16
STREAMS = 8
NT = (((1,), (1,)), ((), ()))
TN = (((0,), (0,)), ((), ()))


def dot(a, b, dims=(((1,), (0,)), ((), ()))):
    return lax.dot_general(a, b, dims, preferred_element_type=F32)


def thirds(x):
    hi = x.astype(BF16).astype(F32)
    mid = (x - hi).astype(BF16).astype(F32)
    return hi, mid, x - hi - mid


def decay_tile(totals):
    row = lax.broadcasted_iota(jnp.int32, (16, HD), 0)
    tile = jnp.zeros((16, HD), F32)
    for h, total in enumerate(totals):
        for j, part in enumerate(thirds(total)):
            tile = jnp.where(row == 3 * h + j, part, tile)
    return tile.astype(BF16)


def read_decay(tile):
    t = tile.astype(F32)
    return [t[3 * h : 3 * h + 1] + t[3 * h + 1 : 3 * h + 2] + t[3 * h + 2 : 3 * h + 3] for h in range(HEADS)]


def per_head(pair):
    row = lax.broadcasted_iota(jnp.int32, (BODY, HD), 0)
    return jnp.where(row < SLICE, pair[0], pair[1])


def kernel(
    nx, ny,
    q_in, k_in, v_in, ld_in, gain_in, w_ref, res_ref, out_ref,
    q_ref, k_ref, v_ref, ld_ref, gain_ref, wbuf, resbuf, sbuf, abuf, xsend, xbuf, psend, pbuf, att, grown, nbuf, nrecv, part, rbuf,
    load_sem, core_send, core_recv, a_send, a_recv, x_send, x_recv, p_send, p_recv, ring_send, ring_recv,
):
    ctx, ex = lax.axis_index("ctx"), lax.axis_index("exp")
    x, z = ctx // NZ, lax.rem(ctx, NZ)
    y, core = ex // 2, lax.rem(ex, 2)
    rows = q_in.shape[0]
    kdim = w_ref.shape[0]
    mate = (ctx, y * 2 + 1 - core)
    up = (ctx, lax.rem(y + 1, ny) * 2 + core)
    down = (ctx, lax.rem(y + ny - 1, ny) * 2 + core)

    def z_peer(j):
        return lax.rem(z + j, NZ)

    def x_peer(j):
        return lax.rem(x + j, nx)

    loads = [
        pltpu.make_async_copy(a, b, load_sem.at[2 + i])
        for i, (a, b) in enumerate(
            ((ld_in, ld_ref), (k_in, k_ref), (v_in, v_ref), (q_in, q_ref), (gain_in, gain_ref))
        )
    ]
    for load in loads:
        load.start()
    load_w = pltpu.make_async_copy(w_ref, wbuf.at[pl.ds(0, kdim)], load_sem.at[0])
    load_w.start()
    load_res = pltpu.make_async_copy(res_ref, resbuf, load_sem.at[1])
    load_res.start()

    barrier = pltpu.get_barrier_semaphore()
    peers = [(x * NZ + z_peer(j), ex) for j in range(1, NZ)]
    peers += [(x_peer(j) * NZ + z, ex) for j in range(1, nx)]
    peers += [up, down, mate]
    for peer in peers:
        pl.semaphore_signal(barrier, inc=1, device_id=peer, device_id_type=MESH)

    loads[0].wait()
    ld = jnp.concatenate([ld_ref[...]] * (8 // HEADS), axis=0)
    hi, mid, lo = thirds(ld)
    kind = lax.broadcasted_iota(jnp.int32, ld.shape, 0) // HEADS
    parts = jnp.where(kind == 0, hi, jnp.where(kind == 1, mid, jnp.where(kind == 2, lo, 0.0))).astype(BF16)
    ti = lax.broadcasted_iota(jnp.int32, (rows, rows), 0)
    si = lax.broadcasted_iota(jnp.int32, (rows, rows), 1)
    tri = jnp.where(si <= ti, 1.0, 0.0).astype(BF16)
    by_col = dot(tri, parts, NT)
    by_row = dot(parts, tri, NT)
    cum_col = [by_col[:, h : h + 1] + by_col[:, 2 + h : 3 + h] + by_col[:, 4 + h : 5 + h] for h in range(HEADS)]
    cum_row = [by_row[h : h + 1] + by_row[2 + h : 3 + h] + by_row[4 + h : 5 + h] for h in range(HEADS)]
    total = [jnp.broadcast_to(c[rows - 1 : rows], (1, HD)) for c in cum_col]
    for h in range(HEADS):
        grown[:, h : h + 1] = jnp.exp(cum_col[h])

    tile = decay_tile(total)
    loads[1].wait()
    loads[2].wait()
    for h in range(HEADS):
        cols = slice(h * HD, (h + 1) * HD)
        keyed = (k_ref[:, cols].astype(F32) * jnp.exp(total[h] - cum_col[h])).astype(BF16)
        state = dot(keyed, v_ref[:, cols], TN)
        sbuf[:, h * SLICE : (h + 1) * SLICE, :] = state.astype(BF16).reshape(NZ, SLICE, HD)
    for j in range(NZ):
        sbuf[j, BODY:MSG, :] = tile

    pl.semaphore_wait(barrier, len(peers))

    def a_copy(j):
        return pltpu.make_async_remote_copy(
            sbuf.at[z_peer(j)], abuf.at[z], a_send.at[j], a_recv.at[j],
            device_id=(x * NZ + z_peer(j), ex), device_id_type=MESH,
        )

    def x_copy(j):
        return pltpu.make_async_remote_copy(
            xsend, xbuf.at[x], x_send.at[j], x_recv.at[j],
            device_id=(x_peer(j) * NZ + z, ex), device_id_type=MESH,
        )

    def p_copy(j):
        return pltpu.make_async_remote_copy(
            psend.at[z_peer(j)], pbuf.at[z], p_send.at[j], p_recv.at[j],
            device_id=(x * NZ + z_peer(j), ex), device_id_type=MESH,
        )

    for j in range(1, NZ):
        a_copy(j).start()
    w_copy = pltpu.make_async_remote_copy(
        w_ref, wbuf.at[pl.ds(kdim, kdim)], core_send.at[0], core_recv.at[0], device_id=mate, device_id_type=MESH
    )
    w_copy.start()
    abuf[z] = sbuf[z]

    def attend(h, i):
        cols = slice(h * HD, (h + 1) * HD)
        r0, end = i * HD, (i + 1) * HD
        scores = dot(q_ref[r0:end, cols], k_ref[:end, cols], NT)
        spread = cum_col[h][r0:end] - cum_row[h][:, :end]
        at = lax.broadcasted_iota(jnp.int32, (HD, end), 0) + r0
        seen = lax.broadcasted_iota(jnp.int32, (HD, end), 1) <= at
        weight = jnp.exp(jnp.where(seen, spread, -1e30))
        att[r0:end, cols] = dot((scores * weight).astype(BF16), v_ref[:end, cols])

    loads[3].wait()
    loads[4].wait()
    for i in range(rows // HD):
        attend(0, i)

    for j in range(1, NZ):
        a_copy(j).wait_recv()
    state = jnp.zeros((BODY, HD), F32)
    run = [jnp.zeros((1, HD), F32)] * HEADS
    inner, passed = [], []
    for j in range(NZ):
        inner.append(state)
        passed.append(run)
        own = read_decay(abuf[j, BODY:MSG, :])
        state = state * jnp.exp(per_head(own)) + abuf[j, :BODY, :].astype(F32)
        run = [a + b for a, b in zip(run, own)]
    xsend[:BODY, :] = state.astype(BF16)
    xsend[BODY:, :] = decay_tile(run)
    for j in range(1, nx):
        x_copy(j).start()
    xbuf[x] = xsend[...]

    for i in range(rows // HD - 1):
        attend(1, i)

    for j in range(1, nx):
        x_copy(j).wait_recv()
    base = jnp.zeros((BODY, HD), F32)
    for j in range(nx - 1):
        own = read_decay(xbuf[j, BODY:MSG, :])
        later = base * jnp.exp(per_head(own)) + xbuf[j, :BODY, :].astype(F32)
        base = jnp.where(j < x, later, base)
    for j in range(NZ):
        psend[j] = (inner[j] + base * jnp.exp(per_head(passed[j]))).astype(BF16)
    for j in range(1, NZ):
        p_copy(j).start()
    pbuf[z] = psend[z]

    attend(1, rows // HD - 1)

    for j in range(1, NZ):
        p_copy(j).wait_recv()

    far = ny // 2
    order = [far, far - 1, 1 - far]
    for r in range(far - 2, 0, -1):
        order += [r, -r]
    order.append(0)
    place = {r % ny: i for i, r in enumerate(order)}
    near = rows // ny
    mine = near // 2
    wide = part.shape[-1]
    state_in = [pbuf[:, h * SLICE : (h + 1) * SLICE, :].reshape(HD, HD) for h in range(HEADS)]

    def n_copy(g):
        p = pl.ds(groups[g][0], groups[g][1])
        return pltpu.make_async_remote_copy(
            nbuf.at[p, 1 - core], nrecv.at[p], core_send.at[1 + g], core_recv.at[1 + g],
            device_id=mate, device_id_type=MESH,
        )

    def norm(g):
        start, count = groups[g]
        at = [pl.ds(pl.multiple_of(lax.rem(y + r + ny, ny) * near, near), near) for r in order[start : start + count]]
        up_to = jnp.concatenate([grown[a] for a in at], axis=0)
        for h in range(HEADS):
            cols = slice(h * HD, (h + 1) * HD)
            query = jnp.concatenate([q_ref[a, cols] for a in at], axis=0)
            local = jnp.concatenate([att[a, cols] for a in at], axis=0)
            whole = local + dot(query, state_in[h]) * up_to[:, h : h + 1]
            mean = jnp.mean(whole * whole, axis=-1, keepdims=True)
            normed = whole * lax.rsqrt(mean + 1e-6) * gain_ref[:, cols]
            nbuf[start : start + count, :, :, cols] = normed.astype(BF16).reshape(count, 2, mine, HD)
        n_copy(g).start()

    def project(g, b, lhs):
        start, count = groups[g]
        c0 = column(b)
        part[b, start : start + count] = dot(lhs, wbuf[:, c0 : c0 + wide]).astype(BF16).reshape(count, mine, wide)

    def lhs_of(g):
        start, count = groups[g]
        n_copy(g).wait_recv()
        own = nbuf[start : start + count, core].reshape(count * mine, kdim)
        other = nrecv[start : start + count].reshape(count * mine, kdim)
        return jnp.concatenate([own, other], axis=1)

    def column(b):
        return ((b % 2) * (STREAMS // 2) + b // 2) * wide

    def hops(b, upward):
        return far if (b % 2 == 0) == upward else far - 1

    def owed(b, upward, hop):
        left = hops(b, upward) - hop
        return place[(left if upward else -left) % ny]

    def slot(b, upward, hop):
        return hop if upward else hops(b, True) + hop

    def chain(b, upward, hop):
        source = part.at[b, owed(b, upward, hop)] if hop == 0 else rbuf.at[b, slot(b, upward, hop - 1)]
        at = slot(b, upward, hop)
        return pltpu.make_async_remote_copy(
            source, rbuf.at[b, at], ring_send.at[b, at], ring_recv.at[b, at],
            device_id=up if upward else down, device_id_type=MESH,
        )

    groups = [(0, 3), (3, ny - 3)]
    norm(0)
    norm(1)
    load_w.wait()
    w_copy.wait_recv()
    lhs = lhs_of(0)
    for b in range(STREAMS):
        project(0, b, lhs)
        for upward in (True, False):
            chain(b, upward, 0).start()
    lhs = lhs_of(1)
    for b in range(STREAMS):
        project(1, b, lhs)

    for hop in range(1, far):
        for b in range(STREAMS):
            for upward in (True, False):
                if hop < hops(b, upward):
                    chain(b, upward, hop - 1).wait_recv()
                    at = slot(b, upward, hop - 1)
                    own = part[b, owed(b, upward, hop)].astype(F32)
                    rbuf[b, at] = (rbuf[b, at].astype(F32) + own).astype(BF16)
                    chain(b, upward, hop).start()

    load_res.wait()
    for b in range(STREAMS):
        c0 = column(b)
        summed = resbuf[:, c0 : c0 + wide].astype(F32) + part[b, place[0]].astype(F32)
        for upward in (True, False):
            last = hops(b, upward) - 1
            chain(b, upward, last).wait_recv()
            summed += rbuf[b, slot(b, upward, last)].astype(F32)
        out_ref[:, c0 : c0 + wide] = summed.astype(BF16)

    for j in range(1, NZ):
        a_copy(j).wait_send()
        p_copy(j).wait_send()
    for j in range(1, nx):
        x_copy(j).wait_send()
    w_copy.wait_send()
    for g in range(len(groups)):
        n_copy(g).wait_send()
    for b in range(STREAMS):
        for upward in (True, False):
            for hop in range(hops(b, upward)):
                chain(b, upward, hop).wait_send()


def solution(mesh):
    nx, ny = mesh.shape["ctx"] // NZ, mesh.shape["exp"] // 2

    def shards(q_spikes, k_spikes, v_spikes, log_decay, norm_gain, out_weight, residual):
        rows = q_spikes.shape[0]
        kdim, width = out_weight.shape
        mine = residual.shape[0]
        wide = width // STREAMS
        vmem = pl.BlockSpec(memory_space=pltpu.VMEM)
        hbm = pl.BlockSpec(memory_space=pltpu.HBM)
        dma = pltpu.SemaphoreType.DMA
        args = (q_spikes, k_spikes, v_spikes, log_decay.T, norm_gain.reshape(1, -1), out_weight, residual)
        return pl.pallas_call(
            functools.partial(kernel, nx, ny),
            out_shape=pltpu.VMEM(residual.shape, BF16),
            in_specs=[hbm] * 7,
            out_specs=vmem,
            scratch_shapes=[
                pltpu.VMEM(q_spikes.shape, BF16),
                pltpu.VMEM(q_spikes.shape, BF16),
                pltpu.VMEM(q_spikes.shape, BF16),
                pltpu.VMEM((HEADS, rows), F32),
                pltpu.VMEM((1, kdim), F32),
                pltpu.VMEM((2 * kdim, width), BF16),
                pltpu.VMEM((mine, width), BF16),
                pltpu.VMEM((NZ, MSG, HD), BF16),
                pltpu.VMEM((NZ, MSG, HD), BF16),
                pltpu.VMEM((MSG, HD), BF16),
                pltpu.VMEM((nx, MSG, HD), BF16),
                pltpu.VMEM((NZ, BODY, HD), BF16),
                pltpu.VMEM((NZ, BODY, HD), BF16),
                pltpu.VMEM((rows, HEADS * HD), F32),
                pltpu.VMEM((rows, HD), F32),
                pltpu.VMEM((ny, 2, mine, kdim), BF16),
                pltpu.VMEM((ny, mine, kdim), BF16),
                pltpu.VMEM((STREAMS, ny, mine, wide), BF16),
                pltpu.VMEM((STREAMS, ny - 1, mine, wide), BF16),
                dma((7,)), dma((3,)), dma((3,)), dma((NZ,)), dma((NZ,)), dma((nx,)), dma((nx,)),
                dma((NZ,)), dma((NZ,)), dma((STREAMS, ny - 1)), dma((STREAMS, ny - 1)),
            ],
            compiler_params=pltpu.CompilerParams(
                collective_id=0, has_side_effects=True, vmem_limit_bytes=48 * 2**20
            ),
        )(*[pltpu.with_memory_space_constraint(a, pltpu.HBM) for a in args])

    return jax.shard_map(
        shards,
        mesh=mesh,
        in_specs=(
            P("ctx", "exp"),
            P("ctx", "exp"),
            P("ctx", "exp"),
            P("ctx", "exp"),
            P("exp"),
            P("exp", None),
            P(("ctx", "exp"), None),
        ),
        out_specs=P(("ctx", "exp"), None),
        check_vma=False,
    )
```

```python
import functools

import jax
import jax.numpy as jnp
from jax import lax
from jax.experimental import pallas as pl
from jax.experimental.pallas import tpu as pltpu
from jax.sharding import PartitionSpec as P

MESH = pl.DeviceIdType.MESH
F32, BF16 = jnp.float32, jnp.bfloat16
NZ = 8
HEADS, HD = 2, 128
SLICE = HD // NZ
BODY = HEADS * SLICE
MSG = BODY + 16
STREAMS = 4
NT = (((1,), (1,)), ((), ()))
TN = (((0,), (0,)), ((), ()))


def dot(a, b, dims=(((1,), (0,)), ((), ()))):
    return lax.dot_general(a, b, dims, preferred_element_type=F32)


def thirds(x):
    hi = x.astype(BF16).astype(F32)
    mid = (x - hi).astype(BF16).astype(F32)
    return hi, mid, x - hi - mid


def decay_tile(totals):
    row = lax.broadcasted_iota(jnp.int32, (16, HD), 0)
    tile = jnp.zeros((16, HD), F32)
    for h, total in enumerate(totals):
        for j, part in enumerate(thirds(total)):
            tile = jnp.where(row == 3 * h + j, part, tile)
    return tile.astype(BF16)


def read_decay(tile):
    t = tile.astype(F32)
    return [t[3 * h : 3 * h + 1] + t[3 * h + 1 : 3 * h + 2] + t[3 * h + 2 : 3 * h + 3] for h in range(HEADS)]


def per_head(pair):
    row = lax.broadcasted_iota(jnp.int32, (BODY, HD), 0)
    return jnp.where(row < SLICE, pair[0], pair[1])


def kernel(
    nx, ny,
    q_in, k_in, v_in, ld_in, gain_in, w_ref, res_ref, out_ref,
    q_ref, k_ref, v_ref, ld_ref, gain_ref, wbuf, resbuf, sbuf, abuf, xsend, xbuf, psend, pbuf, att, grown, nbuf, nrecv, part, rbuf,
    load_sem, core_send, core_recv, a_send, a_recv, x_send, x_recv, p_send, p_recv, ring_send, ring_recv,
):
    ctx, ex = lax.axis_index("ctx"), lax.axis_index("exp")
    x, z = ctx // NZ, lax.rem(ctx, NZ)
    y, core = ex // 2, lax.rem(ex, 2)
    rows = q_in.shape[0]
    kdim = w_ref.shape[0]
    mate = (ctx, y * 2 + 1 - core)
    up = (ctx, lax.rem(y + 1, ny) * 2 + core)
    down = (ctx, lax.rem(y + ny - 1, ny) * 2 + core)

    def z_peer(j):
        return lax.rem(z + j, NZ)

    def x_peer(j):
        return lax.rem(x + j, nx)

    barrier = pltpu.get_barrier_semaphore()
    peers = [(x * NZ + z_peer(j), ex) for j in sorted(range(1, NZ), key=lambda j: -min(j, NZ - j))]
    peers += [(x_peer(j) * NZ + z, ex) for j in range(1, nx)]
    peers += [up, down, mate]
    for peer in peers:
        pl.semaphore_signal(barrier, inc=1, device_id=peer, device_id_type=MESH)

    loads = [
        pltpu.make_async_copy(a, b, load_sem.at[2 + i])
        for i, (a, b) in enumerate(
            ((ld_in, ld_ref), (k_in, k_ref), (v_in, v_ref), (q_in, q_ref), (gain_in, gain_ref))
        )
    ]
    for load in loads:
        load.start()
    load_w = pltpu.make_async_copy(w_ref, wbuf.at[pl.ds(0, kdim)], load_sem.at[0])
    load_w.start()
    load_res = pltpu.make_async_copy(res_ref, resbuf, load_sem.at[1])
    load_res.start()

    loads[0].wait()
    ld = jnp.concatenate([ld_ref[...]] * (8 // HEADS), axis=0)
    hi, mid, lo = thirds(ld)
    kind = lax.broadcasted_iota(jnp.int32, ld.shape, 0) // HEADS
    parts = jnp.where(kind == 0, hi, jnp.where(kind == 1, mid, jnp.where(kind == 2, lo, 0.0))).astype(BF16)
    ti = lax.broadcasted_iota(jnp.int32, (rows, rows), 0)
    si = lax.broadcasted_iota(jnp.int32, (rows, rows), 1)
    tri = jnp.where(si <= ti, 1.0, 0.0).astype(BF16)
    by_col = dot(tri, parts, NT)
    by_row = dot(parts, tri, NT)
    cum_col = [by_col[:, h : h + 1] + by_col[:, 2 + h : 3 + h] + by_col[:, 4 + h : 5 + h] for h in range(HEADS)]
    cum_row = [by_row[h : h + 1] + by_row[2 + h : 3 + h] + by_row[4 + h : 5 + h] for h in range(HEADS)]
    total = [jnp.broadcast_to(c[rows - 1 : rows], (1, HD)) for c in cum_col]
    for h in range(HEADS):
        grown[:, h : h + 1] = jnp.exp(cum_col[h])

    tile = decay_tile(total)
    loads[1].wait()
    loads[2].wait()
    for h in range(HEADS):
        cols = slice(h * HD, (h + 1) * HD)
        keyed = (k_ref[:, cols].astype(F32) * jnp.exp(total[h] - cum_col[h])).astype(BF16)
        state = dot(keyed, v_ref[:, cols], TN)
        sbuf[:, h * SLICE : (h + 1) * SLICE, :] = state.astype(BF16).reshape(NZ, SLICE, HD)
    for j in range(NZ):
        sbuf[j, BODY:MSG, :] = tile

    pl.semaphore_wait(barrier, len(peers))

    def a_copy(j):
        return pltpu.make_async_remote_copy(
            sbuf.at[z_peer(j)], abuf.at[z], a_send.at[j], a_recv.at[j],
            device_id=(x * NZ + z_peer(j), ex), device_id_type=MESH,
        )

    def x_copy(j):
        return pltpu.make_async_remote_copy(
            xsend, xbuf.at[x], x_send.at[j], x_recv.at[j],
            device_id=(x_peer(j) * NZ + z, ex), device_id_type=MESH,
        )

    def p_copy(j):
        return pltpu.make_async_remote_copy(
            psend.at[z_peer(j)], pbuf.at[z], p_send.at[j], p_recv.at[j],
            device_id=(x * NZ + z_peer(j), ex), device_id_type=MESH,
        )

    for j in range(1, NZ):
        a_copy(j).start()
    w_copy = pltpu.make_async_remote_copy(
        w_ref, wbuf.at[pl.ds(kdim, kdim)], core_send.at[0], core_recv.at[0], device_id=mate, device_id_type=MESH
    )
    w_copy.start()
    abuf[z] = sbuf[z]

    def attend(h, i):
        cols = slice(h * HD, (h + 1) * HD)
        r0, end = i * HD, (i + 1) * HD
        scores = dot(q_ref[r0:end, cols], k_ref[:end, cols], NT)
        spread = cum_col[h][r0:end] - cum_row[h][:, :end]
        at = lax.broadcasted_iota(jnp.int32, (HD, end), 0) + r0
        seen = lax.broadcasted_iota(jnp.int32, (HD, end), 1) <= at
        weight = jnp.exp(jnp.where(seen, spread, -1e30))
        att[r0:end, cols] = dot((scores * weight).astype(BF16), v_ref[:end, cols])

    loads[3].wait()
    loads[4].wait()
    for i in range(rows // HD):
        attend(0, i)

    for j in range(1, NZ):
        a_copy(j).wait_recv()
    state = jnp.zeros((BODY, HD), F32)
    run = [jnp.zeros((1, HD), F32)] * HEADS
    inner, passed = [], []
    for j in range(NZ):
        inner.append(state)
        passed.append(run)
        own = read_decay(abuf[j, BODY:MSG, :])
        state = state * jnp.exp(per_head(own)) + abuf[j, :BODY, :].astype(F32)
        run = [a + b for a, b in zip(run, own)]
    xsend[:BODY, :] = state.astype(BF16)
    xsend[BODY:, :] = decay_tile(run)
    for j in range(1, nx):
        x_copy(j).start()
    xbuf[x] = xsend[...]

    for i in range(rows // HD - 1):
        attend(1, i)

    for j in range(1, nx):
        x_copy(j).wait_recv()
    base = jnp.zeros((BODY, HD), F32)
    for j in range(nx - 1):
        own = read_decay(xbuf[j, BODY:MSG, :])
        later = base * jnp.exp(per_head(own)) + xbuf[j, :BODY, :].astype(F32)
        base = jnp.where(j < x, later, base)
    for j in range(NZ):
        psend[j] = (inner[j] + base * jnp.exp(per_head(passed[j]))).astype(BF16)
    for j in range(1, NZ):
        p_copy(j).start()
    pbuf[z] = psend[z]

    attend(1, rows // HD - 1)

    for j in range(1, NZ):
        p_copy(j).wait_recv()

    far = ny // 2
    order = [far, far - 1, 1 - far]
    for r in range(far - 2, 0, -1):
        order += [r, -r]
    order.append(0)
    place = {r % ny: i for i, r in enumerate(order)}
    near = rows // ny
    mine = near // 2
    wide = part.shape[-1]
    state_in = [pbuf[:, h * SLICE : (h + 1) * SLICE, :].reshape(HD, HD) for h in range(HEADS)]

    def n_copy(g):
        p = pl.ds(groups[g][0], groups[g][1])
        return pltpu.make_async_remote_copy(
            nbuf.at[p, 1 - core], nrecv.at[p], core_send.at[1 + g], core_recv.at[1 + g],
            device_id=mate, device_id_type=MESH,
        )

    def norm(g):
        start, count = groups[g]
        at = [pl.ds(pl.multiple_of(lax.rem(y + r + ny, ny) * near, near), near) for r in order[start : start + count]]
        up_to = jnp.concatenate([grown[a] for a in at], axis=0)
        for h in range(HEADS):
            cols = slice(h * HD, (h + 1) * HD)
            query = jnp.concatenate([q_ref[a, cols] for a in at], axis=0)
            local = jnp.concatenate([att[a, cols] for a in at], axis=0)
            whole = local + dot(query, state_in[h]) * up_to[:, h : h + 1]
            mean = jnp.mean(whole * whole, axis=-1, keepdims=True)
            normed = whole * lax.rsqrt(mean + 1e-6) * gain_ref[:, cols]
            nbuf[start : start + count, :, :, cols] = normed.astype(BF16).reshape(count, 2, mine, HD)
        n_copy(g).start()

    def project(g, b, lhs):
        start, count = groups[g]
        c0 = column(b)
        part[index(b), start : start + count] = dot(lhs, wbuf[:, pl.ds(c0, wide)]).astype(BF16).reshape(count, mine, wide)

    def lhs_of(g):
        start, count = groups[g]
        n_copy(g).wait_recv()
        own = nbuf[start : start + count, core].reshape(count * mine, kdim)
        other = nrecv[start : start + count].reshape(count * mine, kdim)
        return jnp.concatenate([own, other], axis=1)

    def column(b):
        pair, half = b
        c0 = half * (STREAMS // 2) * wide
        return c0 + pair * wide if isinstance(pair, int) else pl.multiple_of(c0 + pair * wide, wide)

    def index(b):
        return b[0] * 2 + b[1]

    def hops(b, upward):
        return far if (b[1] == 0) == upward else far - 1

    def owed(b, upward, hop):
        left = hops(b, upward) - hop
        return place[(left if upward else -left) % ny]

    def slot(b, upward, hop):
        return hop if upward else hops(b, True) + hop

    def chain(b, upward, hop):
        source = part.at[index(b), owed(b, upward, hop)] if hop == 0 else rbuf.at[index(b), slot(b, upward, hop - 1)]
        at = slot(b, upward, hop)
        return pltpu.make_async_remote_copy(
            source, rbuf.at[index(b), at], ring_send.at[index(b), at], ring_recv.at[index(b), at],
            device_id=up if upward else down, device_id_type=MESH,
        )

    def each(body):
        def step(pair, carry):
            for half in (0, 1):
                body((pair, half))
            return carry

        lax.fori_loop(0, STREAMS // 2, step, 0)

    groups = [(0, 3), (3, ny - 3)]
    norm(0)
    norm(1)
    load_w.wait()
    w_copy.wait_recv()
    lhs = lhs_of(0)

    def first(b):
        project(0, b, lhs)
        for upward in (True, False):
            chain(b, upward, 0).start()

    each(first)
    rest = lhs_of(1)
    each(lambda b: project(1, b, rest))

    for hop in range(1, far):

        def pass_on(b, hop=hop):
            for upward in (True, False):
                if hop < hops(b, upward):
                    chain(b, upward, hop - 1).wait_recv()
                    at = slot(b, upward, hop - 1)
                    own = part[index(b), owed(b, upward, hop)].astype(F32)
                    rbuf[index(b), at] = (rbuf[index(b), at].astype(F32) + own).astype(BF16)
                    chain(b, upward, hop).start()

        each(pass_on)

    load_res.wait()

    def finish(b):
        at = pl.ds(column(b), wide)
        summed = resbuf[:, at].astype(F32) + part[index(b), place[0]].astype(F32)
        for upward in (True, False):
            last = hops(b, upward) - 1
            chain(b, upward, last).wait_recv()
            summed += rbuf[index(b), slot(b, upward, last)].astype(F32)
        out_ref[:, at] = summed.astype(BF16)

    each(finish)

    for j in range(1, NZ):
        a_copy(j).wait_send()
        p_copy(j).wait_send()
    for j in range(1, nx):
        x_copy(j).wait_send()
    w_copy.wait_send()
    for g in range(len(groups)):
        n_copy(g).wait_send()

    def drain(b):
        for upward in (True, False):
            for hop in range(hops(b, upward)):
                chain(b, upward, hop).wait_send()

    each(drain)


def solution(mesh):
    nx, ny = mesh.shape["ctx"] // NZ, mesh.shape["exp"] // 2

    def shards(q_spikes, k_spikes, v_spikes, log_decay, norm_gain, out_weight, residual):
        rows = q_spikes.shape[0]
        kdim, width = out_weight.shape
        mine = residual.shape[0]
        wide = width // STREAMS
        vmem = pl.BlockSpec(memory_space=pltpu.VMEM)
        hbm = pl.BlockSpec(memory_space=pltpu.HBM)
        dma = pltpu.SemaphoreType.DMA
        args = (q_spikes, k_spikes, v_spikes, log_decay.T, norm_gain.reshape(1, -1), out_weight, residual)
        return pl.pallas_call(
            functools.partial(kernel, nx, ny),
            out_shape=pltpu.VMEM(residual.shape, BF16),
            in_specs=[hbm] * 7,
            out_specs=vmem,
            scratch_shapes=[
                pltpu.VMEM(q_spikes.shape, BF16),
                pltpu.VMEM(q_spikes.shape, BF16),
                pltpu.VMEM(q_spikes.shape, BF16),
                pltpu.VMEM((HEADS, rows), F32),
                pltpu.VMEM((1, kdim), F32),
                pltpu.VMEM((2 * kdim, width), BF16),
                pltpu.VMEM((mine, width), BF16),
                pltpu.VMEM((NZ, MSG, HD), BF16),
                pltpu.VMEM((NZ, MSG, HD), BF16),
                pltpu.VMEM((MSG, HD), BF16),
                pltpu.VMEM((nx, MSG, HD), BF16),
                pltpu.VMEM((NZ, BODY, HD), BF16),
                pltpu.VMEM((NZ, BODY, HD), BF16),
                pltpu.VMEM((rows, HEADS * HD), F32),
                pltpu.VMEM((rows, HD), F32),
                pltpu.VMEM((ny, 2, mine, kdim), BF16),
                pltpu.VMEM((ny, mine, kdim), BF16),
                pltpu.VMEM((STREAMS, ny, mine, wide), BF16),
                pltpu.VMEM((STREAMS, ny - 1, mine, wide), BF16),
                dma((7,)), dma((3,)), dma((3,)), dma((NZ,)), dma((NZ,)), dma((nx,)), dma((nx,)),
                dma((NZ,)), dma((NZ,)), dma((STREAMS, ny - 1)), dma((STREAMS, ny - 1)),
            ],
            compiler_params=pltpu.CompilerParams(
                collective_id=0, has_side_effects=True, vmem_limit_bytes=48 * 2**20
            ),
        )(*[pltpu.with_memory_space_constraint(a, pltpu.HBM) for a in args])

    return jax.shard_map(
        shards,
        mesh=mesh,
        in_specs=(
            P("ctx", "exp"),
            P("ctx", "exp"),
            P("ctx", "exp"),
            P("ctx", "exp"),
            P("exp"),
            P("exp", None),
            P(("ctx", "exp"), None),
        ),
        out_specs=P(("ctx", "exp"), None),
        check_vma=False,
    )
```

```python
import functools

import jax
import jax.numpy as jnp
from jax import lax
from jax.experimental import pallas as pl
from jax.experimental.pallas import tpu as pltpu
from jax.sharding import PartitionSpec as P

MESH = pl.DeviceIdType.MESH
F32, BF16 = jnp.float32, jnp.bfloat16
NZ = 8
HEADS, HD = 2, 128
SLICE = HD // NZ
BODY = HEADS * SLICE
MSG = BODY + 16
EARLY = 2
STREAMS = 4
NT = (((1,), (1,)), ((), ()))
TN = (((0,), (0,)), ((), ()))


def dot(a, b, dims=(((1,), (0,)), ((), ()))):
    return lax.dot_general(a, b, dims, preferred_element_type=F32)


def thirds(x):
    hi = x.astype(BF16).astype(F32)
    mid = (x - hi).astype(BF16).astype(F32)
    return hi, mid, x - hi - mid


def decay_tile(totals):
    row = lax.broadcasted_iota(jnp.int32, (16, HD), 0)
    tile = jnp.zeros((16, HD), F32)
    for h, total in enumerate(totals):
        for j, part in enumerate(thirds(total)):
            tile = jnp.where(row == 3 * h + j, part, tile)
    return tile.astype(BF16)


def read_decay(tile):
    t = tile.astype(F32)
    return [t[3 * h : 3 * h + 1] + t[3 * h + 1 : 3 * h + 2] + t[3 * h + 2 : 3 * h + 3] for h in range(HEADS)]


def per_head(pair):
    row = lax.broadcasted_iota(jnp.int32, (BODY, HD), 0)
    return jnp.where(row < SLICE, pair[0], pair[1])


def kernel(
    nx, ny,
    q_in, k_in, v_in, ld_in, gain_in, w_ref, res_ref, out_ref,
    q_ref, k_ref, v_ref, ld_ref, gain_ref, wbuf, resbuf, sbuf, abuf, xsend, xbuf, psend, pbuf, direct, entering, att, grown, nbuf, nrecv, part, rbuf,
    load_sem, core_send, core_recv, a_send, a_recv, x_send, x_recv, p_send, p_recv, r_send, r_recv, ring_send, ring_recv,
):
    ctx, ex = lax.axis_index("ctx"), lax.axis_index("exp")
    x, z = ctx // NZ, lax.rem(ctx, NZ)
    y, core = ex // 2, lax.rem(ex, 2)
    rows = q_in.shape[0]
    kdim = w_ref.shape[0]
    mate = (ctx, y * 2 + 1 - core)
    up = (ctx, lax.rem(y + 1, ny) * 2 + core)
    down = (ctx, lax.rem(y + ny - 1, ny) * 2 + core)

    def z_peer(j):
        return lax.rem(z + j, NZ)

    def x_peer(j):
        return lax.rem(x + j, nx)

    barrier = pltpu.get_barrier_semaphore()
    peers = [(x * NZ + z_peer(j), ex) for j in sorted(range(1, NZ), key=lambda j: -min(j, NZ - j))]
    peers += [(x_peer(j) * NZ + z, ex) for j in range(1, nx)]
    peers += [up, down, mate]
    for peer in peers:
        pl.semaphore_signal(barrier, inc=1, device_id=peer, device_id_type=MESH)

    early = z < EARLY

    def greet(c, carry):
        @pl.when(lax.rem(c, NZ) != z)
        def _():
            pl.semaphore_signal(barrier, inc=1, device_id=(c, ex), device_id_type=MESH)

        return carry

    @pl.when(early)
    def _():
        lax.fori_loop(0, x * NZ, greet, 0)

    directs = (nx - 1 - x) * EARLY
    greeted = (nx - 1 - x) * (EARLY - early.astype(jnp.int32))

    loads = [
        pltpu.make_async_copy(a, b, load_sem.at[2 + i])
        for i, (a, b) in enumerate(
            ((ld_in, ld_ref), (k_in, k_ref), (v_in, v_ref), (q_in, q_ref), (gain_in, gain_ref))
        )
    ]
    for load in loads:
        load.start()
    load_w = pltpu.make_async_copy(w_ref, wbuf.at[pl.ds(0, kdim)], load_sem.at[0])
    load_w.start()
    load_res = pltpu.make_async_copy(res_ref, resbuf, load_sem.at[1])
    load_res.start()

    loads[0].wait()
    ld = jnp.concatenate([ld_ref[...]] * (8 // HEADS), axis=0)
    hi, mid, lo = thirds(ld)
    kind = lax.broadcasted_iota(jnp.int32, ld.shape, 0) // HEADS
    parts = jnp.where(kind == 0, hi, jnp.where(kind == 1, mid, jnp.where(kind == 2, lo, 0.0))).astype(BF16)
    ti = lax.broadcasted_iota(jnp.int32, (rows, rows), 0)
    si = lax.broadcasted_iota(jnp.int32, (rows, rows), 1)
    tri = jnp.where(si <= ti, 1.0, 0.0).astype(BF16)
    by_col = dot(tri, parts, NT)
    by_row = dot(parts, tri, NT)
    cum_col = [by_col[:, h : h + 1] + by_col[:, 2 + h : 3 + h] + by_col[:, 4 + h : 5 + h] for h in range(HEADS)]
    cum_row = [by_row[h : h + 1] + by_row[2 + h : 3 + h] + by_row[4 + h : 5 + h] for h in range(HEADS)]
    total = [jnp.broadcast_to(c[rows - 1 : rows], (1, HD)) for c in cum_col]
    for h in range(HEADS):
        grown[:, h : h + 1] = jnp.exp(cum_col[h])

    tile = decay_tile(total)
    loads[1].wait()
    loads[2].wait()
    for h in range(HEADS):
        cols = slice(h * HD, (h + 1) * HD)
        keyed = (k_ref[:, cols].astype(F32) * jnp.exp(total[h] - cum_col[h])).astype(BF16)
        state = dot(keyed, v_ref[:, cols], TN)
        sbuf[:, h * SLICE : (h + 1) * SLICE, :] = state.astype(BF16).reshape(NZ, SLICE, HD)
    for j in range(NZ):
        sbuf[j, BODY:MSG, :] = tile

    pl.semaphore_wait(barrier, len(peers) + greeted)

    def a_copy(j):
        return pltpu.make_async_remote_copy(
            sbuf.at[z_peer(j)], abuf.at[z], a_send.at[j], a_recv.at[j],
            device_id=(x * NZ + z_peer(j), ex), device_id_type=MESH,
        )

    def x_copy(j):
        return pltpu.make_async_remote_copy(
            xsend, xbuf.at[x], x_send.at[j], x_recv.at[j],
            device_id=(x_peer(j) * NZ + z, ex), device_id_type=MESH,
        )

    def p_copy(to):
        return pltpu.make_async_remote_copy(
            psend.at[to], pbuf.at[z], p_send.at[to], p_recv.at[z],
            device_id=(x * NZ + to, ex), device_id_type=MESH,
        )

    def p_wait(source):
        pltpu.make_async_remote_copy(
            psend.at[source], pbuf.at[source], p_send.at[source], p_recv.at[source],
            device_id=(x * NZ + source, ex), device_id_type=MESH,
        ).wait_recv()

    def others(indices, body):
        for i in indices:
            pl.when(z != i)(functools.partial(body, i))

    def r_copy(t):
        to = (x + 1 + t // EARLY) * NZ + lax.rem(t, EARLY)
        return pltpu.make_async_remote_copy(
            xsend, direct.at[ctx], r_send.at[t], r_recv.at[ctx], device_id=(to, ex), device_id_type=MESH
        )

    def r_wait(c):
        pltpu.make_async_remote_copy(
            xsend, direct.at[c], r_send.at[0], r_recv.at[c], device_id=(c, ex), device_id_type=MESH
        ).wait_recv()

    def count(body):
        def step(i, carry):
            body(i)
            return carry

        return step

    for j in range(1, NZ):
        a_copy(j).start()
    w_copy = pltpu.make_async_remote_copy(
        w_ref, wbuf.at[pl.ds(kdim, kdim)], core_send.at[0], core_recv.at[0], device_id=mate, device_id_type=MESH
    )
    w_copy.start()
    abuf[z] = sbuf[z]

    def attend(h, i):
        cols = slice(h * HD, (h + 1) * HD)
        r0, end = i * HD, (i + 1) * HD
        scores = dot(q_ref[r0:end, cols], k_ref[:end, cols], NT)
        spread = cum_col[h][r0:end] - cum_row[h][:, :end]
        at = lax.broadcasted_iota(jnp.int32, (HD, end), 0) + r0
        seen = lax.broadcasted_iota(jnp.int32, (HD, end), 1) <= at
        weight = jnp.exp(jnp.where(seen, spread, -1e30))
        att[r0:end, cols] = dot((scores * weight).astype(BF16), v_ref[:end, cols])

    loads[3].wait()
    loads[4].wait()
    for i in range(rows // HD):
        attend(0, i)

    for j in range(1, NZ):
        a_copy(j).wait_recv()
    state = jnp.zeros((BODY, HD), F32)
    run = [jnp.zeros((1, HD), F32)] * HEADS
    inner, passed, row_decay = [], [], []
    for j in range(NZ):
        inner.append(state)
        passed.append(run)
        own = read_decay(abuf[j, BODY:MSG, :])
        row_decay.append(own)
        state = state * jnp.exp(per_head(own)) + abuf[j, :BODY, :].astype(F32)
        run = [a + b for a, b in zip(run, own)]
    xsend[:BODY, :] = state.astype(BF16)
    xsend[BODY:, :] = decay_tile(run)
    lax.fori_loop(0, directs, count(lambda t: r_copy(t).start()), 0)
    for j in range(EARLY):
        psend[j] = inner[j].astype(BF16)
    others(range(EARLY), lambda i: p_copy(i).start())
    for j in range(1, nx):
        x_copy(j).start()
    xbuf[x] = xsend[...]

    for i in range(rows // HD - 1):
        attend(1, i)

    for j in range(1, nx):
        x_copy(j).wait_recv()
    base = jnp.zeros((BODY, HD), F32)
    for j in range(nx - 1):
        own = read_decay(xbuf[j, BODY:MSG, :])
        later = base * jnp.exp(per_head(own)) + xbuf[j, :BODY, :].astype(F32)
        base = jnp.where(j < x, later, base)
    for j in range(EARLY, NZ):
        psend[j] = (inner[j] + base * jnp.exp(per_head(passed[j]))).astype(BF16)
    others(range(EARLY, NZ), lambda i: p_copy(i).start())
    pbuf[z] = psend[z]

    attend(1, rows // HD - 1)

    others(range(NZ), p_wait)

    @pl.when(early)
    def _():
        lax.fori_loop(0, x * NZ, count(r_wait), 0)
        since = per_head([sum(jnp.where(j < z, own[h], 0.0) for j, own in enumerate(row_decay)) for h in range(HEADS)])
        entering[...] = jnp.zeros_like(entering)

        def join(row):
            own = jnp.exp(per_head(read_decay(direct[row * NZ, BODY:MSG, :])))
            for j in range(NZ):
                entering[j] = entering[j] * own + direct[row * NZ + j, :BODY, :].astype(F32)

        lax.fori_loop(0, x, count(join), 0)
        factor = jnp.exp(since)
        for j in range(NZ):
            pbuf[j] = (pbuf[j].astype(F32) + entering[j] * factor).astype(BF16)

    far = ny // 2
    order = [far, far - 1, 1 - far]
    for r in range(far - 2, 0, -1):
        order += [r, -r]
    order.append(0)
    place = {r % ny: i for i, r in enumerate(order)}
    near = rows // ny
    mine = near // 2
    wide = part.shape[-1]
    state_in = [pbuf[:, h * SLICE : (h + 1) * SLICE, :].reshape(HD, HD) for h in range(HEADS)]

    def n_copy(g):
        p = pl.ds(groups[g][0], groups[g][1])
        return pltpu.make_async_remote_copy(
            nbuf.at[p, 1 - core], nrecv.at[p], core_send.at[1 + g], core_recv.at[1 + g],
            device_id=mate, device_id_type=MESH,
        )

    def norm(g):
        start, count = groups[g]
        at = [pl.ds(pl.multiple_of(lax.rem(y + r + ny, ny) * near, near), near) for r in order[start : start + count]]
        up_to = jnp.concatenate([grown[a] for a in at], axis=0)
        for h in range(HEADS):
            cols = slice(h * HD, (h + 1) * HD)
            query = jnp.concatenate([q_ref[a, cols] for a in at], axis=0)
            local = jnp.concatenate([att[a, cols] for a in at], axis=0)
            whole = local + dot(query, state_in[h]) * up_to[:, h : h + 1]
            mean = jnp.mean(whole * whole, axis=-1, keepdims=True)
            normed = whole * lax.rsqrt(mean + 1e-6) * gain_ref[:, cols]
            nbuf[start : start + count, :, :, cols] = normed.astype(BF16).reshape(count, 2, mine, HD)
        n_copy(g).start()

    def project(g, b, lhs):
        start, count = groups[g]
        c0 = column(b)
        part[index(b), start : start + count] = dot(lhs, wbuf[:, pl.ds(c0, wide)]).astype(BF16).reshape(count, mine, wide)

    def lhs_of(g):
        start, count = groups[g]
        n_copy(g).wait_recv()
        own = nbuf[start : start + count, core].reshape(count * mine, kdim)
        other = nrecv[start : start + count].reshape(count * mine, kdim)
        return jnp.concatenate([own, other], axis=1)

    def column(b):
        pair, half = b
        c0 = half * (STREAMS // 2) * wide
        return c0 + pair * wide if isinstance(pair, int) else pl.multiple_of(c0 + pair * wide, wide)

    def index(b):
        return b[0] * 2 + b[1]

    def hops(b, upward):
        return far if (b[1] == 0) == upward else far - 1

    def owed(b, upward, hop):
        left = hops(b, upward) - hop
        return place[(left if upward else -left) % ny]

    def slot(b, upward, hop):
        return hop if upward else hops(b, True) + hop

    def chain(b, upward, hop):
        source = part.at[index(b), owed(b, upward, hop)] if hop == 0 else rbuf.at[index(b), slot(b, upward, hop - 1)]
        at = slot(b, upward, hop)
        return pltpu.make_async_remote_copy(
            source, rbuf.at[index(b), at], ring_send.at[index(b), at], ring_recv.at[index(b), at],
            device_id=up if upward else down, device_id_type=MESH,
        )

    def each(body):
        def step(pair, carry):
            for half in (0, 1):
                body((pair, half))
            return carry

        lax.fori_loop(0, STREAMS // 2, step, 0)

    groups = [(0, 3), (3, ny - 3)]
    norm(0)
    norm(1)
    load_w.wait()
    w_copy.wait_recv()
    lhs = lhs_of(0)

    def first(b):
        project(0, b, lhs)
        for upward in (True, False):
            chain(b, upward, 0).start()

    each(first)
    rest = lhs_of(1)
    each(lambda b: project(1, b, rest))

    for hop in range(1, far):

        def pass_on(b, hop=hop):
            for upward in (True, False):
                if hop < hops(b, upward):
                    chain(b, upward, hop - 1).wait_recv()
                    at = slot(b, upward, hop - 1)
                    own = part[index(b), owed(b, upward, hop)].astype(F32)
                    rbuf[index(b), at] = (rbuf[index(b), at].astype(F32) + own).astype(BF16)
                    chain(b, upward, hop).start()

        each(pass_on)

    load_res.wait()

    def finish(b):
        at = pl.ds(column(b), wide)
        summed = resbuf[:, at].astype(F32) + part[index(b), place[0]].astype(F32)
        for upward in (True, False):
            last = hops(b, upward) - 1
            chain(b, upward, last).wait_recv()
            summed += rbuf[index(b), slot(b, upward, last)].astype(F32)
        out_ref[:, at] = summed.astype(BF16)

    each(finish)

    for j in range(1, NZ):
        a_copy(j).wait_send()
    others(range(NZ), lambda i: p_copy(i).wait_send())
    lax.fori_loop(0, directs, count(lambda t: r_copy(t).wait_send()), 0)
    for j in range(1, nx):
        x_copy(j).wait_send()
    w_copy.wait_send()
    for g in range(len(groups)):
        n_copy(g).wait_send()

    def drain(b):
        for upward in (True, False):
            for hop in range(hops(b, upward)):
                chain(b, upward, hop).wait_send()

    each(drain)


def solution(mesh):
    nx, ny = mesh.shape["ctx"] // NZ, mesh.shape["exp"] // 2

    def shards(q_spikes, k_spikes, v_spikes, log_decay, norm_gain, out_weight, residual):
        rows = q_spikes.shape[0]
        kdim, width = out_weight.shape
        mine = residual.shape[0]
        wide = width // STREAMS
        vmem = pl.BlockSpec(memory_space=pltpu.VMEM)
        hbm = pl.BlockSpec(memory_space=pltpu.HBM)
        dma = pltpu.SemaphoreType.DMA
        args = (q_spikes, k_spikes, v_spikes, log_decay.T, norm_gain.reshape(1, -1), out_weight, residual)
        return pl.pallas_call(
            functools.partial(kernel, nx, ny),
            out_shape=pltpu.VMEM(residual.shape, BF16),
            in_specs=[hbm] * 7,
            out_specs=vmem,
            scratch_shapes=[
                pltpu.VMEM(q_spikes.shape, BF16),
                pltpu.VMEM(q_spikes.shape, BF16),
                pltpu.VMEM(q_spikes.shape, BF16),
                pltpu.VMEM((HEADS, rows), F32),
                pltpu.VMEM((1, kdim), F32),
                pltpu.VMEM((2 * kdim, width), BF16),
                pltpu.VMEM((mine, width), BF16),
                pltpu.VMEM((NZ, MSG, HD), BF16),
                pltpu.VMEM((NZ, MSG, HD), BF16),
                pltpu.VMEM((MSG, HD), BF16),
                pltpu.VMEM((nx, MSG, HD), BF16),
                pltpu.VMEM((NZ, BODY, HD), BF16),
                pltpu.VMEM((NZ, BODY, HD), BF16),
                pltpu.VMEM(((nx - 1) * NZ, MSG, HD), BF16),
                pltpu.VMEM((NZ, BODY, HD), F32),
                pltpu.VMEM((rows, HEADS * HD), F32),
                pltpu.VMEM((rows, HD), F32),
                pltpu.VMEM((ny, 2, mine, kdim), BF16),
                pltpu.VMEM((ny, mine, kdim), BF16),
                pltpu.VMEM((STREAMS, ny, mine, wide), BF16),
                pltpu.VMEM((STREAMS, ny - 1, mine, wide), BF16),
                dma((7,)), dma((3,)), dma((3,)), dma((NZ,)), dma((NZ,)), dma((nx,)), dma((nx,)),
                dma((NZ,)), dma((NZ,)), dma(((nx - 1) * EARLY,)), dma(((nx - 1) * NZ,)), dma((STREAMS, ny - 1)), dma((STREAMS, ny - 1)),
            ],
            compiler_params=pltpu.CompilerParams(
                collective_id=0, has_side_effects=True, vmem_limit_bytes=48 * 2**20
            ),
        )(*[pltpu.with_memory_space_constraint(a, pltpu.HBM) for a in args])

    return jax.shard_map(
        shards,
        mesh=mesh,
        in_specs=(
            P("ctx", "exp"),
            P("ctx", "exp"),
            P("ctx", "exp"),
            P("ctx", "exp"),
            P("exp"),
            P("exp", None),
            P(("ctx", "exp"), None),
        ),
        out_specs=P(("ctx", "exp"), None),
        check_vma=False,
    )
```

```python
import functools

import jax
import jax.numpy as jnp
from jax import lax
from jax.experimental import pallas as pl
from jax.experimental.pallas import tpu as pltpu
from jax.sharding import PartitionSpec as P

MESH = pl.DeviceIdType.MESH
F32, BF16 = jnp.float32, jnp.bfloat16
NZ = 8
HEADS, HD = 2, 128
SLICE = HD // NZ
BODY = HEADS * SLICE
MSG = BODY + 16
EARLY = 2
STREAMS = 4
ABSORB = 1
NT = (((1,), (1,)), ((), ()))
TN = (((0,), (0,)), ((), ()))


def dot(a, b, dims=(((1,), (0,)), ((), ()))):
    return lax.dot_general(a, b, dims, preferred_element_type=F32)


def thirds(x):
    hi = x.astype(BF16).astype(F32)
    mid = (x - hi).astype(BF16).astype(F32)
    return hi, mid, x - hi - mid


def decay_tile(totals):
    row = lax.broadcasted_iota(jnp.int32, (16, HD), 0)
    tile = jnp.zeros((16, HD), F32)
    for h, total in enumerate(totals):
        for j, part in enumerate(thirds(total)):
            tile = jnp.where(row == 3 * h + j, part, tile)
    return tile.astype(BF16)


def read_decay(tile):
    t = tile.astype(F32)
    return [t[3 * h : 3 * h + 1] + t[3 * h + 1 : 3 * h + 2] + t[3 * h + 2 : 3 * h + 3] for h in range(HEADS)]


def per_head(pair):
    row = lax.broadcasted_iota(jnp.int32, (BODY, HD), 0)
    return jnp.where(row < SLICE, pair[0], pair[1])


def kernel(
    nx, ny,
    q_in, k_in, v_in, ld_in, gain_in, w_ref, res_ref, out_ref,
    q_ref, k_ref, v_ref, ld_ref, gain_ref, wbuf, resbuf, sbuf, abuf, xsend, xbuf, psend, pbuf, direct, entering, att, grown, nbuf, nrecv, wnext, head, part, rbuf,
    load_sem, core_send, core_recv, a_send, a_recv, x_send, x_recv, p_send, p_recv, r_send, r_recv, y_send, y_recv, f_send, f_recv, h_send, h_recv, ring_send, ring_recv,
):
    ctx, ex = lax.axis_index("ctx"), lax.axis_index("exp")
    x, z = ctx // NZ, lax.rem(ctx, NZ)
    y, core = ex // 2, lax.rem(ex, 2)
    rows = q_in.shape[0]
    kdim = w_ref.shape[0]
    mate = (ctx, y * 2 + 1 - core)
    up = (ctx, lax.rem(y + 1, ny) * 2 + core)
    down = (ctx, lax.rem(y + ny - 1, ny) * 2 + core)

    aslant = [(ctx, lax.rem(y + d, ny) * 2 + 1 - core) for d in (1, ny - 1)]

    def z_peer(j):
        return lax.rem(z + j, NZ)

    def x_peer(j):
        return lax.rem(x + j, nx)

    barrier = pltpu.get_barrier_semaphore()
    peers = [(x * NZ + z_peer(j), ex) for j in sorted(range(1, NZ), key=lambda j: -min(j, NZ - j))]
    peers += [(x_peer(j) * NZ + z, ex) for j in range(1, nx)]
    peers += [up, down, mate, *aslant]
    for peer in peers:
        pl.semaphore_signal(barrier, inc=1, device_id=peer, device_id_type=MESH)

    early = z < EARLY

    def greet(c, carry):
        @pl.when(lax.rem(c, NZ) != z)
        def _():
            pl.semaphore_signal(barrier, inc=1, device_id=(c, ex), device_id_type=MESH)

        return carry

    @pl.when(early)
    def _():
        lax.fori_loop(0, x * NZ, greet, 0)

    directs = (nx - 1 - x) * EARLY
    greeted = (nx - 1 - x) * (EARLY - early.astype(jnp.int32))

    loads = [
        pltpu.make_async_copy(a, b, load_sem.at[2 + i])
        for i, (a, b) in enumerate(
            ((ld_in, ld_ref), (k_in, k_ref), (v_in, v_ref), (q_in, q_ref), (gain_in, gain_ref))
        )
    ]
    for load in loads:
        load.start()
    load_w = pltpu.make_async_copy(w_ref, wbuf.at[pl.ds(0, kdim)], load_sem.at[0])
    load_w.start()
    load_res = pltpu.make_async_copy(res_ref, resbuf, load_sem.at[1])
    load_res.start()

    loads[0].wait()
    ld = jnp.concatenate([ld_ref[...]] * (8 // HEADS), axis=0)
    hi, mid, lo = thirds(ld)
    kind = lax.broadcasted_iota(jnp.int32, ld.shape, 0) // HEADS
    parts = jnp.where(kind == 0, hi, jnp.where(kind == 1, mid, jnp.where(kind == 2, lo, 0.0))).astype(BF16)
    ti = lax.broadcasted_iota(jnp.int32, (rows, rows), 0)
    si = lax.broadcasted_iota(jnp.int32, (rows, rows), 1)
    tri = jnp.where(si <= ti, 1.0, 0.0).astype(BF16)
    by_col = dot(tri, parts, NT)
    by_row = dot(parts, tri, NT)
    cum_col = [by_col[:, h : h + 1] + by_col[:, 2 + h : 3 + h] + by_col[:, 4 + h : 5 + h] for h in range(HEADS)]
    cum_row = [by_row[h : h + 1] + by_row[2 + h : 3 + h] + by_row[4 + h : 5 + h] for h in range(HEADS)]
    total = [jnp.broadcast_to(c[rows - 1 : rows], (1, HD)) for c in cum_col]
    for h in range(HEADS):
        grown[:, h : h + 1] = jnp.exp(cum_col[h])

    tile = decay_tile(total)
    loads[1].wait()
    loads[2].wait()
    for h in range(HEADS):
        cols = slice(h * HD, (h + 1) * HD)
        keyed = (k_ref[:, cols].astype(F32) * jnp.exp(total[h] - cum_col[h])).astype(BF16)
        state = dot(keyed, v_ref[:, cols], TN)
        sbuf[:, h * SLICE : (h + 1) * SLICE, :] = state.astype(BF16).reshape(NZ, SLICE, HD)
    for j in range(NZ):
        sbuf[j, BODY:MSG, :] = tile

    pl.semaphore_wait(barrier, len(peers) + greeted)

    def a_copy(j):
        return pltpu.make_async_remote_copy(
            sbuf.at[z_peer(j)], abuf.at[z], a_send.at[j], a_recv.at[j],
            device_id=(x * NZ + z_peer(j), ex), device_id_type=MESH,
        )

    def x_copy(j):
        return pltpu.make_async_remote_copy(
            xsend, xbuf.at[x], x_send.at[j], x_recv.at[j],
            device_id=(x_peer(j) * NZ + z, ex), device_id_type=MESH,
        )

    def p_copy(to):
        return pltpu.make_async_remote_copy(
            psend.at[to], pbuf.at[z], p_send.at[to], p_recv.at[z],
            device_id=(x * NZ + to, ex), device_id_type=MESH,
        )

    def p_wait(source):
        pltpu.make_async_remote_copy(
            psend.at[source], pbuf.at[source], p_send.at[source], p_recv.at[source],
            device_id=(x * NZ + source, ex), device_id_type=MESH,
        ).wait_recv()

    def others(indices, body):
        for i in indices:
            pl.when(z != i)(functools.partial(body, i))

    def r_copy(t):
        to = (x + 1 + t // EARLY) * NZ + lax.rem(t, EARLY)
        return pltpu.make_async_remote_copy(
            xsend, direct.at[ctx], r_send.at[t], r_recv.at[ctx], device_id=(to, ex), device_id_type=MESH
        )

    def r_wait(c):
        pltpu.make_async_remote_copy(
            xsend, direct.at[c], r_send.at[0], r_recv.at[c], device_id=(c, ex), device_id_type=MESH
        ).wait_recv()

    def count(body):
        def step(i, carry):
            body(i)
            return carry

        return step

    for j in range(1, NZ):
        a_copy(j).start()
    w_copy = pltpu.make_async_remote_copy(
        w_ref, wbuf.at[pl.ds(kdim, kdim)], core_send.at[0], core_recv.at[0], device_id=mate, device_id_type=MESH
    )
    w_copy.start()
    half_cols = w_ref.shape[1] // 2
    block = half_cols // (STREAMS // 2)

    def y_copy(d, p):
        there = wnext.at[d, pl.ds(0, kdim), pl.ds(p * block, block)]
        return pltpu.make_async_remote_copy(
            w_ref.at[:, pl.ds(d * half_cols + p * block, block)], there, y_send.at[d, p], y_recv.at[d, p],
            device_id=(up, down)[d], device_id_type=MESH,
        )

    def f_copy(d, p):
        cols = pl.ds(p * block, block)
        return pltpu.make_async_remote_copy(
            wnext.at[d, pl.ds(0, kdim), cols], wnext.at[d, pl.ds(kdim, kdim), cols], f_send.at[d, p], f_recv.at[d, p],
            device_id=mate, device_id_type=MESH,
        )

    def hand_on(p):
        for d in (0, 1):
            y_copy(d, p).wait_recv()
            f_copy(d, p).start()

    for p in range(ABSORB):
        for d in (0, 1):
            y_copy(d, p).start()
    abuf[z] = sbuf[z]

    def attend(h, i):
        cols = slice(h * HD, (h + 1) * HD)
        r0, end = i * HD, (i + 1) * HD
        scores = dot(q_ref[r0:end, cols], k_ref[:end, cols], NT)
        spread = cum_col[h][r0:end] - cum_row[h][:, :end]
        at = lax.broadcasted_iota(jnp.int32, (HD, end), 0) + r0
        seen = lax.broadcasted_iota(jnp.int32, (HD, end), 1) <= at
        weight = jnp.exp(jnp.where(seen, spread, -1e30))
        att[r0:end, cols] = dot((scores * weight).astype(BF16), v_ref[:end, cols])

    loads[3].wait()
    loads[4].wait()
    for i in range(rows // HD):
        attend(0, i)

    for j in range(1, NZ):
        a_copy(j).wait_recv()
    state = jnp.zeros((BODY, HD), F32)
    run = [jnp.zeros((1, HD), F32)] * HEADS
    inner, passed, row_decay = [], [], []
    for j in range(NZ):
        inner.append(state)
        passed.append(run)
        own = read_decay(abuf[j, BODY:MSG, :])
        row_decay.append(own)
        state = state * jnp.exp(per_head(own)) + abuf[j, :BODY, :].astype(F32)
        run = [a + b for a, b in zip(run, own)]
    xsend[:BODY, :] = state.astype(BF16)
    xsend[BODY:, :] = decay_tile(run)
    lax.fori_loop(0, directs, count(lambda t: r_copy(t).start()), 0)
    for j in range(EARLY):
        psend[j] = inner[j].astype(BF16)
    others(range(EARLY), lambda i: p_copy(i).start())
    for j in range(1, nx):
        x_copy(j).start()
    xbuf[x] = xsend[...]

    for i in range(rows // HD - 1):
        attend(1, i)

    for j in range(1, nx):
        x_copy(j).wait_recv()
    base = jnp.zeros((BODY, HD), F32)
    for j in range(nx - 1):
        own = read_decay(xbuf[j, BODY:MSG, :])
        later = base * jnp.exp(per_head(own)) + xbuf[j, :BODY, :].astype(F32)
        base = jnp.where(j < x, later, base)
    for j in range(EARLY, NZ):
        psend[j] = (inner[j] + base * jnp.exp(per_head(passed[j]))).astype(BF16)
    others(range(EARLY, NZ), lambda i: p_copy(i).start())
    pbuf[z] = psend[z]

    attend(1, rows // HD - 1)

    others(range(NZ), p_wait)

    @pl.when(early)
    def _():
        lax.fori_loop(0, x * NZ, count(r_wait), 0)
        since = per_head([sum(jnp.where(j < z, own[h], 0.0) for j, own in enumerate(row_decay)) for h in range(HEADS)])
        entering[...] = jnp.zeros_like(entering)

        def join(row):
            own = jnp.exp(per_head(read_decay(direct[row * NZ, BODY:MSG, :])))
            for j in range(NZ):
                entering[j] = entering[j] * own + direct[row * NZ + j, :BODY, :].astype(F32)

        lax.fori_loop(0, x, count(join), 0)
        factor = jnp.exp(since)
        for j in range(NZ):
            pbuf[j] = (pbuf[j].astype(F32) + entering[j] * factor).astype(BF16)

    far = ny // 2
    order = [far, far - 1, 1 - far]
    for r in range(far - 2, 0, -1):
        order += [r, -r]
    order.append(0)
    place = {r % ny: i for i, r in enumerate(order)}
    near = rows // ny
    mine = near // 2
    wide = part.shape[-1]
    state_in = [pbuf[:, h * SLICE : (h + 1) * SLICE, :].reshape(HD, HD) for h in range(HEADS)]

    def n_copy(g):
        p = pl.ds(groups[g][0], groups[g][1])
        return pltpu.make_async_remote_copy(
            nbuf.at[p, 1 - core], nrecv.at[p], core_send.at[1 + g], core_recv.at[1 + g],
            device_id=mate, device_id_type=MESH,
        )

    def norm(g):
        start, count = groups[g]
        at = [pl.ds(pl.multiple_of(lax.rem(y + r + ny, ny) * near, near), near) for r in order[start : start + count]]
        up_to = jnp.concatenate([grown[a] for a in at], axis=0)
        for h in range(HEADS):
            cols = slice(h * HD, (h + 1) * HD)
            query = jnp.concatenate([q_ref[a, cols] for a in at], axis=0)
            local = jnp.concatenate([att[a, cols] for a in at], axis=0)
            whole = local + dot(query, state_in[h]) * up_to[:, h : h + 1]
            mean = jnp.mean(whole * whole, axis=-1, keepdims=True)
            normed = whole * lax.rsqrt(mean + 1e-6) * gain_ref[:, cols]
            nbuf[start : start + count, :, :, cols] = normed.astype(BF16).reshape(count, 2, mine, HD)
        n_copy(g).start()

    def h_copy(d, k):
        return pltpu.make_async_remote_copy(
            nbuf.at[0, lax.rem(core + k, 2)], head.at[d, k], h_send.at[d, k], h_recv.at[d, k],
            device_id=(up, down)[d] if k == 0 else aslant[d], device_id_type=MESH,
        )

    def project(g, b, lhs):
        start, count = groups[g]
        c0 = column(b)
        part[index(b), start : start + count] = dot(lhs, wbuf[:, pl.ds(c0, wide)]).astype(BF16).reshape(count, mine, wide)

    def lhs_of(g):
        start, count = groups[g]
        n_copy(g).wait_recv()
        own = nbuf[start : start + count, core].reshape(count * mine, kdim)
        other = nrecv[start : start + count].reshape(count * mine, kdim)
        return jnp.concatenate([own, other], axis=1)

    def column(b):
        pair, half = b
        c0 = half * (STREAMS // 2) * wide
        return c0 + pair * wide if isinstance(pair, int) else pl.multiple_of(c0 + pair * wide, wide)

    def index(b):
        return b[0] * 2 + b[1]

    def hops(b, upward):
        return far if (b[1] == 0) == upward else far - 1

    def owed(b, upward, hop):
        left = hops(b, upward) - hop
        return place[(left if upward else -left) % ny]

    def slot(b, upward, hop):
        return hop if upward else hops(b, True) + hop

    def chain(b, upward, hop):
        source = part.at[index(b), owed(b, upward, hop)] if hop == 0 else rbuf.at[index(b), slot(b, upward, hop - 1)]
        at = slot(b, upward, hop)
        return pltpu.make_async_remote_copy(
            source, rbuf.at[index(b), at], ring_send.at[index(b), at], ring_recv.at[index(b), at],
            device_id=up if upward else down, device_id_type=MESH,
        )

    def each(body, start=0, end=STREAMS // 2):
        def step(pair, carry):
            for half in (0, 1):
                body((pair, half))
            return carry

        lax.fori_loop(start, end, step, 0)

    groups = [(0, 3), (3, ny - 3)]
    for p in range(ABSORB - 1):
        hand_on(p)
    norm(0)
    for d in (0, 1):
        for k in (0, 1):
            h_copy(d, k).start()
    norm(1)
    load_w.wait()
    w_copy.wait_recv()
    lhs = lhs_of(0)

    def longer(b):
        return b[1] == 0

    def first(b, absorbed):
        project(0, b, lhs)
        for upward in (True, False):
            if not (absorbed and upward == longer(b)):
                chain(b, upward, 0).start()

    each(functools.partial(first, absorbed=True), 0, ABSORB)
    each(functools.partial(first, absorbed=False), ABSORB)
    hand_on(ABSORB - 1)
    rest = lhs_of(1)
    for d in (0, 1):
        for k in (0, 1):
            h_copy(d, k).wait_recv()
    heads = [jnp.concatenate([head[d, 0], head[d, 1]], axis=1) for d in (0, 1)]

    for p in range(ABSORB):
        for d in (0, 1):
            b, upward = (p, d), d == 0
            f_copy(d, p).wait_recv()
            theirs = dot(heads[d], wnext[d, :, p * block : (p + 1) * block])
            own = part[index(b), owed(b, upward, 1)].astype(F32)
            rbuf[index(b), slot(b, upward, 0)] = (theirs + own).astype(BF16)
            chain(b, upward, 1).start()
    each(lambda b: project(1, b, rest))

    def pass_on(b, hop, absorbed):
        for upward in (True, False):
            if hop < hops(b, upward) and not (absorbed and hop == 1 and upward == longer(b)):
                chain(b, upward, hop - 1).wait_recv()
                at = slot(b, upward, hop - 1)
                own = part[index(b), owed(b, upward, hop)].astype(F32)
                rbuf[index(b), at] = (rbuf[index(b), at].astype(F32) + own).astype(BF16)
                chain(b, upward, hop).start()

    for hop in range(1, far):
        each(functools.partial(pass_on, hop=hop, absorbed=True), 0, ABSORB)
        each(functools.partial(pass_on, hop=hop, absorbed=False), ABSORB)

    load_res.wait()

    def finish(b):
        at = pl.ds(column(b), wide)
        summed = resbuf[:, at].astype(F32) + part[index(b), place[0]].astype(F32)
        for upward in (True, False):
            last = hops(b, upward) - 1
            chain(b, upward, last).wait_recv()
            summed += rbuf[index(b), slot(b, upward, last)].astype(F32)
        out_ref[:, at] = summed.astype(BF16)

    each(finish)

    for j in range(1, NZ):
        a_copy(j).wait_send()
    others(range(NZ), lambda i: p_copy(i).wait_send())
    lax.fori_loop(0, directs, count(lambda t: r_copy(t).wait_send()), 0)
    for j in range(1, nx):
        x_copy(j).wait_send()
    w_copy.wait_send()
    for g in range(len(groups)):
        n_copy(g).wait_send()

    for d in (0, 1):
        for p in range(ABSORB):
            y_copy(d, p).wait_send()
            f_copy(d, p).wait_send()
        for k in (0, 1):
            h_copy(d, k).wait_send()

    def drain(b, absorbed):
        for upward in (True, False):
            for hop in range(hops(b, upward)):
                if not (absorbed and hop == 0 and upward == longer(b)):
                    chain(b, upward, hop).wait_send()

    each(functools.partial(drain, absorbed=True), 0, ABSORB)
    each(functools.partial(drain, absorbed=False), ABSORB)


def solution(mesh):
    nx, ny = mesh.shape["ctx"] // NZ, mesh.shape["exp"] // 2

    def shards(q_spikes, k_spikes, v_spikes, log_decay, norm_gain, out_weight, residual):
        rows = q_spikes.shape[0]
        kdim, width = out_weight.shape
        mine = residual.shape[0]
        wide = width // STREAMS
        vmem = pl.BlockSpec(memory_space=pltpu.VMEM)
        hbm = pl.BlockSpec(memory_space=pltpu.HBM)
        dma = pltpu.SemaphoreType.DMA
        args = (q_spikes, k_spikes, v_spikes, log_decay.T, norm_gain.reshape(1, -1), out_weight, residual)
        return pl.pallas_call(
            functools.partial(kernel, nx, ny),
            out_shape=pltpu.VMEM(residual.shape, BF16),
            in_specs=[hbm] * 7,
            out_specs=vmem,
            scratch_shapes=[
                pltpu.VMEM(q_spikes.shape, BF16),
                pltpu.VMEM(q_spikes.shape, BF16),
                pltpu.VMEM(q_spikes.shape, BF16),
                pltpu.VMEM((HEADS, rows), F32),
                pltpu.VMEM((1, kdim), F32),
                pltpu.VMEM((2 * kdim, width), BF16),
                pltpu.VMEM((mine, width), BF16),
                pltpu.VMEM((NZ, MSG, HD), BF16),
                pltpu.VMEM((NZ, MSG, HD), BF16),
                pltpu.VMEM((MSG, HD), BF16),
                pltpu.VMEM((nx, MSG, HD), BF16),
                pltpu.VMEM((NZ, BODY, HD), BF16),
                pltpu.VMEM((NZ, BODY, HD), BF16),
                pltpu.VMEM(((nx - 1) * NZ, MSG, HD), BF16),
                pltpu.VMEM((NZ, BODY, HD), F32),
                pltpu.VMEM((rows, HEADS * HD), F32),
                pltpu.VMEM((rows, HD), F32),
                pltpu.VMEM((ny, 2, mine, kdim), BF16),
                pltpu.VMEM((ny, mine, kdim), BF16),
                pltpu.VMEM((2, 2 * kdim, ABSORB * wide), BF16),
                pltpu.VMEM((2, 2, mine, kdim), BF16),
                pltpu.VMEM((STREAMS, ny, mine, wide), BF16),
                pltpu.VMEM((STREAMS, ny - 1, mine, wide), BF16),
                dma((7,)), dma((3,)), dma((3,)), dma((NZ,)), dma((NZ,)), dma((nx,)), dma((nx,)),
                dma((NZ,)), dma((NZ,)), dma(((nx - 1) * EARLY,)), dma(((nx - 1) * NZ,)), dma((2, ABSORB)), dma((2, ABSORB)), dma((2, ABSORB)), dma((2, ABSORB)), dma((2, 2)), dma((2, 2)),
                dma((STREAMS, ny - 1)), dma((STREAMS, ny - 1)),
            ],
            compiler_params=pltpu.CompilerParams(
                collective_id=0, has_side_effects=True, vmem_limit_bytes=48 * 2**20
            ),
        )(*[pltpu.with_memory_space_constraint(a, pltpu.HBM) for a in args])

    return jax.shard_map(
        shards,
        mesh=mesh,
        in_specs=(
            P("ctx", "exp"),
            P("ctx", "exp"),
            P("ctx", "exp"),
            P("ctx", "exp"),
            P("exp"),
            P("exp", None),
            P(("ctx", "exp"), None),
        ),
        out_specs=P(("ctx", "exp"), None),
        check_vma=False,
    )
```

```python
import functools

import jax
import jax.numpy as jnp
from jax import lax
from jax.experimental import pallas as pl
from jax.experimental.pallas import tpu as pltpu
from jax.sharding import PartitionSpec as P

MESH = pl.DeviceIdType.MESH
F32, BF16 = jnp.float32, jnp.bfloat16
NZ = 8
HEADS, HD = 2, 128
SLICE = HD // NZ
BODY = HEADS * SLICE
MSG = BODY + 16
EARLY = 2
STREAMS = 4
ABSORB = 1
NT = (((1,), (1,)), ((), ()))
TN = (((0,), (0,)), ((), ()))


def dot(a, b, dims=(((1,), (0,)), ((), ()))):
    return lax.dot_general(a, b, dims, preferred_element_type=F32)


def thirds(x):
    hi = x.astype(BF16).astype(F32)
    mid = (x - hi).astype(BF16).astype(F32)
    return hi, mid, x - hi - mid


def decay_tile(totals):
    row = lax.broadcasted_iota(jnp.int32, (16, HD), 0)
    tile = jnp.zeros((16, HD), F32)
    for h, total in enumerate(totals):
        for j, part in enumerate(thirds(total)):
            tile = jnp.where(row == 3 * h + j, part, tile)
    return tile.astype(BF16)


def read_decay(tile):
    t = tile.astype(F32)
    return [t[3 * h : 3 * h + 1] + t[3 * h + 1 : 3 * h + 2] + t[3 * h + 2 : 3 * h + 3] for h in range(HEADS)]


def per_head(pair):
    row = lax.broadcasted_iota(jnp.int32, (BODY, HD), 0)
    return jnp.where(row < SLICE, pair[0], pair[1])


def kernel(
    nx, ny,
    q_in, k_in, v_in, ld_in, gain_in, w_ref, res_ref, out_ref,
    q_ref, kv_ref, ld_ref, gain_ref, wbuf, resbuf, sbuf, abuf, xsend, xbuf, psend, pbuf, direct, entering, att, grown, nbuf, nrecv, wnext, head, part, rbuf,
    load_sem, core_send, core_recv, a_send, a_recv, x_send, x_recv, p_send, p_recv, r_send, r_recv, y_send, y_recv, f_send, f_recv, h_send, h_recv, ring_send, ring_recv,
):
    ctx, ex = lax.axis_index("ctx"), lax.axis_index("exp")
    x, z = ctx // NZ, lax.rem(ctx, NZ)
    y, core = ex // 2, lax.rem(ex, 2)
    rows = q_in.shape[0]
    kdim = w_ref.shape[0]
    mate = (ctx, y * 2 + 1 - core)
    up = (ctx, lax.rem(y + 1, ny) * 2 + core)
    down = (ctx, lax.rem(y + ny - 1, ny) * 2 + core)

    aslant = [(ctx, lax.rem(y + d, ny) * 2 + 1 - core) for d in (1, ny - 1)]

    def await_all(like, sem):
        pltpu.make_async_copy(like, like, sem).wait()

    def z_peer(j):
        return lax.rem(z + j, NZ)

    def x_peer(j):
        return lax.rem(x + j, nx)

    barrier = pltpu.get_barrier_semaphore()
    peers = [(x * NZ + z_peer(j), ex) for j in sorted(range(1, NZ), key=lambda j: -min(j, NZ - j))]
    peers += [(x_peer(j) * NZ + z, ex) for j in range(1, nx)]
    peers += [up, down, mate, *aslant]
    for peer in peers:
        pl.semaphore_signal(barrier, inc=1, device_id=peer, device_id_type=MESH)

    early = z < EARLY

    def greet(c, carry):
        @pl.when(lax.rem(c, NZ) != z)
        def _():
            pl.semaphore_signal(barrier, inc=1, device_id=(c, ex), device_id_type=MESH)

        return carry

    @pl.when(early)
    def _():
        lax.fori_loop(0, x * NZ, greet, 0)

    directs = (nx - 1 - x) * EARLY
    greeted = (nx - 1 - x) * (EARLY - early.astype(jnp.int32))

    k_ref, v_ref = kv_ref.at[0], kv_ref.at[1]
    loads = [
        pltpu.make_async_copy(a, b, load_sem.at[i])
        for a, b, i in (
            (ld_in, ld_ref, 2), (k_in, k_ref, 3), (v_in, v_ref, 3), (q_in, q_ref, 4), (gain_in, gain_ref, 5)
        )
    ]
    for load in loads:
        load.start()
    load_w = pltpu.make_async_copy(w_ref, wbuf.at[pl.ds(0, kdim)], load_sem.at[0])
    load_w.start()
    load_res = pltpu.make_async_copy(res_ref, resbuf, load_sem.at[1])
    load_res.start()

    loads[0].wait()
    ld = jnp.concatenate([ld_ref[...]] * (8 // HEADS), axis=0)
    hi, mid, lo = thirds(ld)
    kind = lax.broadcasted_iota(jnp.int32, ld.shape, 0) // HEADS
    parts = jnp.where(kind == 0, hi, jnp.where(kind == 1, mid, jnp.where(kind == 2, lo, 0.0))).astype(BF16)
    ti = lax.broadcasted_iota(jnp.int32, (rows, rows), 0)
    si = lax.broadcasted_iota(jnp.int32, (rows, rows), 1)
    tri = jnp.where(si <= ti, 1.0, 0.0).astype(BF16)
    by_col = dot(tri, parts, NT)
    by_row = dot(parts, tri, NT)
    cum_col = [by_col[:, h : h + 1] + by_col[:, 2 + h : 3 + h] + by_col[:, 4 + h : 5 + h] for h in range(HEADS)]
    cum_row = [by_row[h : h + 1] + by_row[2 + h : 3 + h] + by_row[4 + h : 5 + h] for h in range(HEADS)]
    total = [jnp.broadcast_to(c[rows - 1 : rows], (1, HD)) for c in cum_col]
    for h in range(HEADS):
        grown[:, h : h + 1] = jnp.exp(cum_col[h])

    tile = decay_tile(total)
    await_all(kv_ref, load_sem.at[3])
    for h in range(HEADS):
        cols = slice(h * HD, (h + 1) * HD)
        keyed = (k_ref[:, cols].astype(F32) * jnp.exp(total[h] - cum_col[h])).astype(BF16)
        state = dot(keyed, v_ref[:, cols], TN)
        sbuf[:, h * SLICE : (h + 1) * SLICE, :] = state.astype(BF16).reshape(NZ, SLICE, HD)
    for j in range(NZ):
        sbuf[j, BODY:MSG, :] = tile

    pl.semaphore_wait(barrier, len(peers) + greeted)

    def a_copy(j):
        return pltpu.make_async_remote_copy(
            sbuf.at[z_peer(j)], abuf.at[z], a_send, a_recv,
            device_id=(x * NZ + z_peer(j), ex), device_id_type=MESH,
        )

    def x_copy(j):
        return pltpu.make_async_remote_copy(
            xsend, xbuf.at[x], x_send, x_recv,
            device_id=(x_peer(j) * NZ + z, ex), device_id_type=MESH,
        )

    def p_copy(to):
        return pltpu.make_async_remote_copy(
            psend.at[to], pbuf.at[z], p_send, p_recv,
            device_id=(x * NZ + to, ex), device_id_type=MESH,
        )

    def others(indices, body):
        for i in indices:
            pl.when(z != i)(functools.partial(body, i))

    def r_copy(t):
        to = (x + 1 + t // EARLY) * NZ + lax.rem(t, EARLY)
        return pltpu.make_async_remote_copy(
            xsend, direct.at[ctx], r_send.at[t // EARLY], r_recv.at[x], device_id=(to, ex), device_id_type=MESH
        )

    def count(body):
        def step(i, carry):
            body(i)
            return carry

        return step

    for j in range(1, NZ):
        a_copy(j).start()
    w_copy = pltpu.make_async_remote_copy(
        w_ref, wbuf.at[pl.ds(kdim, kdim)], core_send.at[0], core_recv.at[0], device_id=mate, device_id_type=MESH
    )
    w_copy.start()
    half_cols = w_ref.shape[1] // 2
    block = half_cols // (STREAMS // 2)

    def y_copy(d, p):
        there = wnext.at[d, pl.ds(0, kdim), pl.ds(p * block, block)]
        return pltpu.make_async_remote_copy(
            w_ref.at[:, pl.ds(d * half_cols + p * block, block)], there, y_send, y_recv,
            device_id=(up, down)[d], device_id_type=MESH,
        )

    def f_copy(d, p):
        cols = pl.ds(p * block, block)
        return pltpu.make_async_remote_copy(
            wnext.at[d, pl.ds(0, kdim), cols], wnext.at[d, pl.ds(kdim, kdim), cols], f_send, f_recv,
            device_id=mate, device_id_type=MESH,
        )

    def hand_on():
        await_all(wnext.at[:, pl.ds(0, kdim)], y_recv)
        for p in range(ABSORB):
            for d in (0, 1):
                f_copy(d, p).start()

    for p in range(ABSORB):
        for d in (0, 1):
            y_copy(d, p).start()
    abuf[z] = sbuf[z]

    def attend(h, i):
        cols = slice(h * HD, (h + 1) * HD)
        r0, end = i * HD, (i + 1) * HD
        scores = dot(q_ref[r0:end, cols], k_ref[:end, cols], NT)
        spread = cum_col[h][r0:end] - cum_row[h][:, :end]
        at = lax.broadcasted_iota(jnp.int32, (HD, end), 0) + r0
        seen = lax.broadcasted_iota(jnp.int32, (HD, end), 1) <= at
        weight = jnp.exp(jnp.where(seen, spread, -1e30))
        att[r0:end, cols] = dot((scores * weight).astype(BF16), v_ref[:end, cols])

    loads[3].wait()
    loads[4].wait()
    for i in range(rows // HD):
        attend(0, i)

    await_all(abuf.at[pl.ds(0, NZ - 1)], a_recv)
    state = jnp.zeros((BODY, HD), F32)
    run = [jnp.zeros((1, HD), F32)] * HEADS
    inner, passed, row_decay = [], [], []
    for j in range(NZ):
        inner.append(state)
        passed.append(run)
        own = read_decay(abuf[j, BODY:MSG, :])
        row_decay.append(own)
        state = state * jnp.exp(per_head(own)) + abuf[j, :BODY, :].astype(F32)
        run = [a + b for a, b in zip(run, own)]
    xsend[:BODY, :] = state.astype(BF16)
    xsend[BODY:, :] = decay_tile(run)
    lax.fori_loop(0, directs, count(lambda t: r_copy(t).start()), 0)
    for j in range(EARLY):
        psend[j] = inner[j].astype(BF16)
    others(range(EARLY), lambda i: p_copy(i).start())
    for j in range(1, nx):
        x_copy(j).start()
    xbuf[x] = xsend[...]

    for i in range(rows // HD - 1):
        attend(1, i)

    await_all(xbuf.at[pl.ds(0, nx - 1)], x_recv)
    base = jnp.zeros((BODY, HD), F32)
    for j in range(nx - 1):
        own = read_decay(xbuf[j, BODY:MSG, :])
        later = base * jnp.exp(per_head(own)) + xbuf[j, :BODY, :].astype(F32)
        base = jnp.where(j < x, later, base)
    for j in range(EARLY, NZ):
        psend[j] = (inner[j] + base * jnp.exp(per_head(passed[j]))).astype(BF16)
    others(range(EARLY, NZ), lambda i: p_copy(i).start())
    pbuf[z] = psend[z]

    attend(1, rows // HD - 1)

    await_all(pbuf.at[pl.ds(0, NZ - 1)], p_recv)

    @pl.when(early)
    def _():
        since = per_head([sum(jnp.where(j < z, own[h], 0.0) for j, own in enumerate(row_decay)) for h in range(HEADS)])
        entering[...] = jnp.zeros_like(entering)

        def join(row):
            await_all(direct.at[pl.ds(row * NZ, NZ)], r_recv.at[row])
            own = jnp.exp(per_head(read_decay(direct[row * NZ, BODY:MSG, :])))
            for j in range(NZ):
                entering[j] = entering[j] * own + direct[row * NZ + j, :BODY, :].astype(F32)

        lax.fori_loop(0, x, count(join), 0)
        factor = jnp.exp(since)
        for j in range(NZ):
            pbuf[j] = (pbuf[j].astype(F32) + entering[j] * factor).astype(BF16)

    far = ny // 2
    order = [far, far - 1, 1 - far]
    for r in range(far - 2, 0, -1):
        order += [r, -r]
    order.append(0)
    place = {r % ny: i for i, r in enumerate(order)}
    near = rows // ny
    mine = near // 2
    wide = part.shape[-1]
    state_in = [pbuf[:, h * SLICE : (h + 1) * SLICE, :].reshape(HD, HD) for h in range(HEADS)]

    def n_copy(g):
        p = pl.ds(groups[g][0], groups[g][1])
        return pltpu.make_async_remote_copy(
            nbuf.at[p, 1 - core], nrecv.at[p], core_send.at[1], core_recv.at[1 + g],
            device_id=mate, device_id_type=MESH,
        )

    def norm(g):
        start, count = groups[g]
        at = [pl.ds(pl.multiple_of(lax.rem(y + r + ny, ny) * near, near), near) for r in order[start : start + count]]
        up_to = jnp.concatenate([grown[a] for a in at], axis=0)
        for h in range(HEADS):
            cols = slice(h * HD, (h + 1) * HD)
            query = jnp.concatenate([q_ref[a, cols] for a in at], axis=0)
            local = jnp.concatenate([att[a, cols] for a in at], axis=0)
            whole = local + dot(query, state_in[h]) * up_to[:, h : h + 1]
            mean = jnp.mean(whole * whole, axis=-1, keepdims=True)
            normed = whole * lax.rsqrt(mean + 1e-6) * gain_ref[:, cols]
            nbuf[start : start + count, :, :, cols] = normed.astype(BF16).reshape(count, 2, mine, HD)
        n_copy(g).start()

    def h_copy(d, k):
        return pltpu.make_async_remote_copy(
            nbuf.at[0, lax.rem(core + k, 2)], head.at[d, k], h_send, h_recv,
            device_id=(up, down)[d] if k == 0 else aslant[d], device_id_type=MESH,
        )

    def project(g, b, lhs):
        start, count = groups[g]
        c0 = column(b)
        part[index(b), start : start + count] = dot(lhs, wbuf[:, pl.ds(c0, wide)]).astype(BF16).reshape(count, mine, wide)

    def lhs_of(g):
        start, count = groups[g]
        n_copy(g).wait_recv()
        own = nbuf[start : start + count, core].reshape(count * mine, kdim)
        other = nrecv[start : start + count].reshape(count * mine, kdim)
        return jnp.concatenate([own, other], axis=1)

    def column(b):
        pair, half = b
        c0 = half * (STREAMS // 2) * wide
        return c0 + pair * wide if isinstance(pair, int) else pl.multiple_of(c0 + pair * wide, wide)

    def index(b):
        return b[0] * 2 + b[1]

    def hops(b, upward):
        return far if (b[1] == 0) == upward else far - 1

    def owed(b, upward, hop):
        left = hops(b, upward) - hop
        return place[(left if upward else -left) % ny]

    def slot(b, upward, hop):
        return hop if upward else hops(b, True) + hop

    def chain(b, upward, hop):
        source = part.at[index(b), owed(b, upward, hop)] if hop == 0 else rbuf.at[index(b), slot(b, upward, hop - 1)]
        at = slot(b, upward, hop)
        return pltpu.make_async_remote_copy(
            source, rbuf.at[index(b), at], ring_send, ring_recv.at[index(b), at],
            device_id=up if upward else down, device_id_type=MESH,
        )

    def each(body, start=0, end=STREAMS // 2):
        def step(pair, carry):
            for half in (0, 1):
                body((pair, half))
            return carry

        lax.fori_loop(start, end, step, 0)

    groups = [(0, 3), (3, ny - 3)]
    norm(0)
    for d in (0, 1):
        for k in (0, 1):
            h_copy(d, k).start()
    norm(1)
    load_w.wait()
    w_copy.wait_recv()
    lhs = lhs_of(0)

    def longer(b):
        return b[1] == 0

    def first(b, absorbed):
        project(0, b, lhs)
        for upward in (True, False):
            if not (absorbed and upward == longer(b)):
                chain(b, upward, 0).start()

    each(functools.partial(first, absorbed=True), 0, ABSORB)
    each(functools.partial(first, absorbed=False), ABSORB)
    hand_on()
    rest = lhs_of(1)
    await_all(head, h_recv)
    heads = [jnp.concatenate([head[d, 0], head[d, 1]], axis=1) for d in (0, 1)]

    await_all(wnext.at[:, pl.ds(kdim, kdim)], f_recv)
    for p in range(ABSORB):
        for d in (0, 1):
            b, upward = (p, d), d == 0
            theirs = dot(heads[d], wnext[d, :, p * block : (p + 1) * block])
            own = part[index(b), owed(b, upward, 1)].astype(F32)
            rbuf[index(b), slot(b, upward, 0)] = (theirs + own).astype(BF16)
            chain(b, upward, 1).start()
    each(lambda b: project(1, b, rest))

    def pass_on(b, hop, absorbed):
        for upward in (True, False):
            if hop < hops(b, upward) and not (absorbed and hop == 1 and upward == longer(b)):
                chain(b, upward, hop - 1).wait_recv()
                at = slot(b, upward, hop - 1)
                own = part[index(b), owed(b, upward, hop)].astype(F32)
                rbuf[index(b), at] = (rbuf[index(b), at].astype(F32) + own).astype(BF16)
                chain(b, upward, hop).start()

    for hop in range(1, far):
        each(functools.partial(pass_on, hop=hop, absorbed=True), 0, ABSORB)
        each(functools.partial(pass_on, hop=hop, absorbed=False), ABSORB)

    load_res.wait()

    def finish(b):
        at = pl.ds(column(b), wide)
        summed = resbuf[:, at].astype(F32) + part[index(b), place[0]].astype(F32)
        for upward in (True, False):
            last = hops(b, upward) - 1
            chain(b, upward, last).wait_recv()
            summed += rbuf[index(b), slot(b, upward, last)].astype(F32)
        out_ref[:, at] = summed.astype(BF16)

    each(finish)

    await_all(sbuf.at[pl.ds(0, NZ - 1)], a_send)
    await_all(psend.at[pl.ds(0, NZ - 1)], p_send)
    await_all(xbuf.at[pl.ds(0, nx - 1)], x_send)
    lax.fori_loop(0, nx - 1 - x, count(lambda d: await_all(direct.at[pl.ds(0, EARLY)], r_send.at[d])), 0)
    w_copy.wait_send()
    await_all(nrecv, core_send.at[1])
    await_all(wnext.at[:, pl.ds(0, kdim)], y_send)
    await_all(wnext.at[:, pl.ds(0, kdim)], f_send)
    await_all(head, h_send)
    sent = STREAMS * (ny - 1) - 2 * ABSORB
    await_all(wbuf.at[pl.ds(0, sent * mine // STREAMS)], ring_send)


def solution(mesh):
    nx, ny = mesh.shape["ctx"] // NZ, mesh.shape["exp"] // 2

    def shards(q_spikes, k_spikes, v_spikes, log_decay, norm_gain, out_weight, residual):
        rows = q_spikes.shape[0]
        kdim, width = out_weight.shape
        mine = residual.shape[0]
        wide = width // STREAMS
        vmem = pl.BlockSpec(memory_space=pltpu.VMEM)
        hbm = pl.BlockSpec(memory_space=pltpu.HBM)
        dma = pltpu.SemaphoreType.DMA
        args = (q_spikes, k_spikes, v_spikes, log_decay.T, norm_gain.reshape(1, -1), out_weight, residual)
        return pl.pallas_call(
            functools.partial(kernel, nx, ny),
            out_shape=pltpu.VMEM(residual.shape, BF16),
            in_specs=[hbm] * 7,
            out_specs=vmem,
            scratch_shapes=[
                pltpu.VMEM(q_spikes.shape, BF16),
                pltpu.VMEM((2, *q_spikes.shape), BF16),
                pltpu.VMEM((HEADS, rows), F32),
                pltpu.VMEM((1, kdim), F32),
                pltpu.VMEM((2 * kdim, width), BF16),
                pltpu.VMEM((mine, width), BF16),
                pltpu.VMEM((NZ, MSG, HD), BF16),
                pltpu.VMEM((NZ, MSG, HD), BF16),
                pltpu.VMEM((MSG, HD), BF16),
                pltpu.VMEM((nx, MSG, HD), BF16),
                pltpu.VMEM((NZ, BODY, HD), BF16),
                pltpu.VMEM((NZ, BODY, HD), BF16),
                pltpu.VMEM(((nx - 1) * NZ, MSG, HD), BF16),
                pltpu.VMEM((NZ, BODY, HD), F32),
                pltpu.VMEM((rows, HEADS * HD), F32),
                pltpu.VMEM((rows, HD), F32),
                pltpu.VMEM((ny, 2, mine, kdim), BF16),
                pltpu.VMEM((ny, mine, kdim), BF16),
                pltpu.VMEM((2, 2 * kdim, ABSORB * wide), BF16),
                pltpu.VMEM((2, 2, mine, kdim), BF16),
                pltpu.VMEM((STREAMS, ny, mine, wide), BF16),
                pltpu.VMEM((STREAMS, ny - 1, mine, wide), BF16),
                dma((6,)), dma((2,)), dma((3,)), dma, dma, dma, dma, dma, dma, dma((nx - 1,)), dma((nx - 1,)),
                dma, dma, dma, dma, dma, dma, dma, dma((STREAMS, ny - 1)),
            ],
            compiler_params=pltpu.CompilerParams(
                collective_id=0, has_side_effects=True, vmem_limit_bytes=48 * 2**20
            ),
        )(*[pltpu.with_memory_space_constraint(a, pltpu.HBM) for a in args])

    return jax.shard_map(
        shards,
        mesh=mesh,
        in_specs=(
            P("ctx", "exp"),
            P("ctx", "exp"),
            P("ctx", "exp"),
            P("ctx", "exp"),
            P("exp"),
            P("exp", None),
            P(("ctx", "exp"), None),
        ),
        out_specs=P(("ctx", "exp"), None),
        check_vma=False,
    )
```

```python
import functools

import jax
import jax.numpy as jnp
from jax import lax
from jax.experimental import pallas as pl
from jax.experimental.pallas import tpu as pltpu
from jax.sharding import PartitionSpec as P

MESH = pl.DeviceIdType.MESH
F32, BF16 = jnp.float32, jnp.bfloat16
NZ = 8
HEADS, HD = 2, 128
SLICE = HD // NZ
BODY = HEADS * SLICE
MSG = BODY + 16
EARLY = 2
STREAMS = 4
ABSORB = 1
NT = (((1,), (1,)), ((), ()))
TN = (((0,), (0,)), ((), ()))


def dot(a, b, dims=(((1,), (0,)), ((), ()))):
    return lax.dot_general(a, b, dims, preferred_element_type=F32)


def thirds(x):
    hi = x.astype(BF16).astype(F32)
    mid = (x - hi).astype(BF16).astype(F32)
    return hi, mid, x - hi - mid


def decay_tile(totals):
    row = lax.broadcasted_iota(jnp.int32, (16, HD), 0)
    tile = jnp.zeros((16, HD), F32)
    for h, total in enumerate(totals):
        for j, part in enumerate(thirds(total)):
            tile = jnp.where(row == 3 * h + j, part, tile)
    return tile.astype(BF16)


def read_decay(tile):
    t = tile.astype(F32)
    return [t[3 * h : 3 * h + 1] + t[3 * h + 1 : 3 * h + 2] + t[3 * h + 2 : 3 * h + 3] for h in range(HEADS)]


def per_head(pair):
    row = lax.broadcasted_iota(jnp.int32, (BODY, HD), 0)
    return jnp.where(row < SLICE, pair[0], pair[1])


def kernel(
    nx, ny,
    q_in, k_in, v_in, ld_in, gain_in, w_ref, res_ref, out_ref,
    q_ref, kv_ref, ld_ref, gain_ref, wbuf, resbuf, sbuf, abuf, xsend, xbuf, psend, pbuf, direct, entering, att, grown, nbuf, nrecv, wnext, head, part, rbuf,
    load_sem, core_send, core_recv, a_send, a_recv, x_send, x_recv, p_send, p_recv, r_send, r_recv, y_send, y_recv, f_send, f_recv, h_send, h_recv, ring_send, ring_recv,
):
    ctx, ex = lax.axis_index("ctx"), lax.axis_index("exp")
    x, z = ctx // NZ, lax.rem(ctx, NZ)
    y, core = ex // 2, lax.rem(ex, 2)
    rows = q_in.shape[0]
    kdim = w_ref.shape[0]
    mate = (ctx, y * 2 + 1 - core)
    up = (ctx, lax.rem(y + 1, ny) * 2 + core)
    down = (ctx, lax.rem(y + ny - 1, ny) * 2 + core)

    aslant = [(ctx, lax.rem(y + d, ny) * 2 + 1 - core) for d in (1, ny - 1)]

    def await_all(like, sem):
        pltpu.make_async_copy(like, like, sem).wait()

    def z_peer(j):
        return lax.rem(z + j, NZ)

    def x_peer(j):
        return lax.rem(x + j, nx)

    barrier = pltpu.get_barrier_semaphore()
    peers = [(x * NZ + z_peer(j), ex) for j in sorted(range(1, NZ), key=lambda j: -min(j, NZ - j))]
    peers += [(x_peer(j) * NZ + z, ex) for j in range(1, nx)]
    peers += [up, down, mate, *aslant]
    for peer in peers:
        pl.semaphore_signal(barrier, inc=1, device_id=peer, device_id_type=MESH)

    early = z < EARLY

    def greet(c, carry):
        @pl.when(lax.rem(c, NZ) != z)
        def _():
            pl.semaphore_signal(barrier, inc=1, device_id=(c, ex), device_id_type=MESH)

        return carry

    @pl.when(early)
    def _():
        lax.fori_loop(0, x * NZ, greet, 0)

    directs = (nx - 1 - x) * EARLY
    greeted = (nx - 1 - x) * (EARLY - early.astype(jnp.int32))

    k_ref, v_ref = kv_ref.at[0], kv_ref.at[1]
    loads = [
        pltpu.make_async_copy(a, b, load_sem.at[i])
        for a, b, i in (
            (ld_in, ld_ref, 2), (k_in, k_ref, 3), (v_in, v_ref, 3), (q_in, q_ref, 4), (gain_in, gain_ref, 5)
        )
    ]
    for load in loads:
        load.start()
    load_w = pltpu.make_async_copy(w_ref, wbuf.at[pl.ds(0, kdim)], load_sem.at[0])
    load_w.start()
    load_res = pltpu.make_async_copy(res_ref, resbuf, load_sem.at[1])
    load_res.start()

    loads[0].wait()
    ld = jnp.concatenate([ld_ref[...]] * (8 // HEADS), axis=0)
    hi, mid, lo = thirds(ld)
    kind = lax.broadcasted_iota(jnp.int32, ld.shape, 0) // HEADS
    parts = jnp.where(kind == 0, hi, jnp.where(kind == 1, mid, jnp.where(kind == 2, lo, 0.0))).astype(BF16)
    ti = lax.broadcasted_iota(jnp.int32, (rows, rows), 0)
    si = lax.broadcasted_iota(jnp.int32, (rows, rows), 1)
    tri = jnp.where(si <= ti, 1.0, 0.0).astype(BF16)
    by_col = dot(tri, parts, NT)
    by_row = dot(parts, tri, NT)
    cum_col = [by_col[:, h : h + 1] + by_col[:, 2 + h : 3 + h] + by_col[:, 4 + h : 5 + h] for h in range(HEADS)]
    cum_row = [by_row[h : h + 1] + by_row[2 + h : 3 + h] + by_row[4 + h : 5 + h] for h in range(HEADS)]
    total = [jnp.broadcast_to(c[rows - 1 : rows], (1, HD)) for c in cum_col]
    for h in range(HEADS):
        grown[:, h : h + 1] = jnp.exp(cum_col[h])

    tile = decay_tile(total)
    await_all(kv_ref, load_sem.at[3])
    for h in range(HEADS):
        cols = slice(h * HD, (h + 1) * HD)
        keyed = (k_ref[:, cols].astype(F32) * jnp.exp(total[h] - cum_col[h])).astype(BF16)
        state = dot(keyed, v_ref[:, cols], TN)
        sbuf[:, h * SLICE : (h + 1) * SLICE, :] = state.astype(BF16).reshape(NZ, SLICE, HD)
    for j in range(NZ):
        sbuf[j, BODY:MSG, :] = tile

    pl.semaphore_wait(barrier, len(peers) + greeted)

    def a_copy(j):
        return pltpu.make_async_remote_copy(
            sbuf.at[z_peer(j)], abuf.at[z], a_send, a_recv,
            device_id=(x * NZ + z_peer(j), ex), device_id_type=MESH,
        )

    def x_copy(j):
        return pltpu.make_async_remote_copy(
            xsend, xbuf.at[x], x_send, x_recv,
            device_id=(x_peer(j) * NZ + z, ex), device_id_type=MESH,
        )

    def p_copy(to):
        return pltpu.make_async_remote_copy(
            psend.at[to], pbuf.at[z], p_send, p_recv,
            device_id=(x * NZ + to, ex), device_id_type=MESH,
        )

    def others(indices, body):
        for i in indices:
            pl.when(z != i)(functools.partial(body, i))

    def r_copy(t):
        to = (x + 1 + t // EARLY) * NZ + lax.rem(t, EARLY)
        return pltpu.make_async_remote_copy(
            xsend.at[pl.ds(0, BODY)], direct.at[ctx], r_send.at[t // EARLY], r_recv.at[x], device_id=(to, ex), device_id_type=MESH
        )

    def count(body):
        def step(i, carry):
            body(i)
            return carry

        return step

    for j in range(1, NZ):
        a_copy(j).start()
    w_copy = pltpu.make_async_remote_copy(
        w_ref, wbuf.at[pl.ds(kdim, kdim)], core_send.at[0], core_recv.at[0], device_id=mate, device_id_type=MESH
    )
    w_copy.start()
    half_cols = w_ref.shape[1] // 2
    block = half_cols // (STREAMS // 2)

    def y_copy(d, p):
        there = wnext.at[d, pl.ds(0, kdim), pl.ds(p * block, block)]
        return pltpu.make_async_remote_copy(
            w_ref.at[:, pl.ds(d * half_cols + p * block, block)], there, y_send, y_recv,
            device_id=(up, down)[d], device_id_type=MESH,
        )

    def f_copy(d, p):
        cols = pl.ds(p * block, block)
        return pltpu.make_async_remote_copy(
            wnext.at[d, pl.ds(0, kdim), cols], wnext.at[d, pl.ds(kdim, kdim), cols], f_send, f_recv,
            device_id=mate, device_id_type=MESH,
        )

    def hand_on():
        await_all(wnext.at[:, pl.ds(0, kdim)], y_recv)
        for p in range(ABSORB):
            for d in (0, 1):
                f_copy(d, p).start()

    for p in range(ABSORB):
        for d in (0, 1):
            y_copy(d, p).start()
    abuf[z] = sbuf[z]

    def attend(h, i):
        cols = slice(h * HD, (h + 1) * HD)
        r0, end = i * HD, (i + 1) * HD
        scores = dot(q_ref[r0:end, cols], k_ref[:end, cols], NT)
        spread = cum_col[h][r0:end] - cum_row[h][:, :end]
        at = lax.broadcasted_iota(jnp.int32, (HD, end), 0) + r0
        seen = lax.broadcasted_iota(jnp.int32, (HD, end), 1) <= at
        weight = jnp.exp(jnp.where(seen, spread, -1e30))
        att[r0:end, cols] = dot((scores * weight).astype(BF16), v_ref[:end, cols])

    loads[3].wait()
    loads[4].wait()
    for i in range(rows // HD):
        attend(0, i)

    await_all(abuf.at[pl.ds(0, NZ - 1)], a_recv)
    state = jnp.zeros((BODY, HD), F32)
    run = [jnp.zeros((1, HD), F32)] * HEADS
    inner, passed, row_decay = [], [], []
    for j in range(NZ):
        inner.append(state)
        passed.append(run)
        own = read_decay(abuf[j, BODY:MSG, :])
        row_decay.append(own)
        state = state * jnp.exp(per_head(own)) + abuf[j, :BODY, :].astype(F32)
        run = [a + b for a, b in zip(run, own)]
    xsend[:BODY, :] = state.astype(BF16)
    xsend[BODY:, :] = decay_tile(run)
    lax.fori_loop(0, directs, count(lambda t: r_copy(t).start()), 0)
    for j in range(EARLY):
        psend[j] = inner[j].astype(BF16)
    others(range(EARLY), lambda i: p_copy(i).start())
    for j in range(1, nx):
        x_copy(j).start()
    xbuf[x] = xsend[...]

    for i in range(rows // HD - 1):
        attend(1, i)

    await_all(xbuf.at[pl.ds(0, nx - 1)], x_recv)
    base = jnp.zeros((BODY, HD), F32)
    for j in range(nx - 1):
        own = read_decay(xbuf[j, BODY:MSG, :])
        later = base * jnp.exp(per_head(own)) + xbuf[j, :BODY, :].astype(F32)
        base = jnp.where(j < x, later, base)
    for j in range(EARLY, NZ):
        psend[j] = (inner[j] + base * jnp.exp(per_head(passed[j]))).astype(BF16)
    others(range(EARLY, NZ), lambda i: p_copy(i).start())
    pbuf[z] = psend[z]

    attend(1, rows // HD - 1)

    await_all(pbuf.at[pl.ds(0, NZ - 1)], p_recv)

    @pl.when(early)
    def _():
        since = per_head([sum(jnp.where(j < z, own[h], 0.0) for j, own in enumerate(row_decay)) for h in range(HEADS)])
        entering[...] = jnp.zeros_like(entering)

        def join(row):
            await_all(direct.at[pl.ds(row * NZ, NZ)], r_recv.at[row])
            own = jnp.exp(per_head(read_decay(xbuf[row, BODY:MSG, :])))
            for j in range(NZ):
                entering[j] = entering[j] * own + direct[row * NZ + j].astype(F32)

        lax.fori_loop(0, x, count(join), 0)
        factor = jnp.exp(since)
        for j in range(NZ):
            pbuf[j] = (pbuf[j].astype(F32) + entering[j] * factor).astype(BF16)

    far = ny // 2
    order = [far, far - 1, 1 - far]
    for r in range(far - 2, 0, -1):
        order += [r, -r]
    order.append(0)
    place = {r % ny: i for i, r in enumerate(order)}
    near = rows // ny
    mine = near // 2
    wide = part.shape[-1]
    state_in = [pbuf[:, h * SLICE : (h + 1) * SLICE, :].reshape(HD, HD) for h in range(HEADS)]

    def n_copy(g):
        p = pl.ds(groups[g][0], groups[g][1])
        return pltpu.make_async_remote_copy(
            nbuf.at[p, 1 - core], nrecv.at[p], core_send.at[1], core_recv.at[1 + g],
            device_id=mate, device_id_type=MESH,
        )

    def norm(g):
        start, count = groups[g]
        at = [pl.ds(pl.multiple_of(lax.rem(y + r + ny, ny) * near, near), near) for r in order[start : start + count]]
        up_to = jnp.concatenate([grown[a] for a in at], axis=0)
        for h in range(HEADS):
            cols = slice(h * HD, (h + 1) * HD)
            query = jnp.concatenate([q_ref[a, cols] for a in at], axis=0)
            local = jnp.concatenate([att[a, cols] for a in at], axis=0)
            whole = local + dot(query, state_in[h]) * up_to[:, h : h + 1]
            mean = jnp.mean(whole * whole, axis=-1, keepdims=True)
            normed = whole * lax.rsqrt(mean + 1e-6) * gain_ref[:, cols]
            nbuf[start : start + count, :, :, cols] = normed.astype(BF16).reshape(count, 2, mine, HD)
        n_copy(g).start()

    def h_copy(d, k):
        return pltpu.make_async_remote_copy(
            nbuf.at[0, lax.rem(core + k, 2)], head.at[d, k], h_send, h_recv,
            device_id=(up, down)[d] if k == 0 else aslant[d], device_id_type=MESH,
        )

    def project(g, b, lhs):
        start, count = groups[g]
        c0 = column(b)
        part[index(b), start : start + count] = dot(lhs, wbuf[:, pl.ds(c0, wide)]).astype(BF16).reshape(count, mine, wide)

    def lhs_of(g):
        start, count = groups[g]
        n_copy(g).wait_recv()
        own = nbuf[start : start + count, core].reshape(count * mine, kdim)
        other = nrecv[start : start + count].reshape(count * mine, kdim)
        return jnp.concatenate([own, other], axis=1)

    def column(b):
        pair, half = b
        c0 = half * (STREAMS // 2) * wide
        return c0 + pair * wide if isinstance(pair, int) else pl.multiple_of(c0 + pair * wide, wide)

    def index(b):
        return b[0] * 2 + b[1]

    def hops(b, upward):
        return far if (b[1] == 0) == upward else far - 1

    def owed(b, upward, hop):
        left = hops(b, upward) - hop
        return place[(left if upward else -left) % ny]

    def slot(b, upward, hop):
        return hop if upward else hops(b, True) + hop

    def chain(b, upward, hop):
        source = part.at[index(b), owed(b, upward, hop)] if hop == 0 else rbuf.at[index(b), slot(b, upward, hop - 1)]
        at = slot(b, upward, hop)
        return pltpu.make_async_remote_copy(
            source, rbuf.at[index(b), at], ring_send, ring_recv.at[index(b), at],
            device_id=up if upward else down, device_id_type=MESH,
        )

    def each(body, start=0, end=STREAMS // 2):
        def step(pair, carry):
            for half in (0, 1):
                body((pair, half))
            return carry

        lax.fori_loop(start, end, step, 0)

    groups = [(0, 3), (3, ny - 3)]
    norm(0)
    for d in (0, 1):
        for k in (0, 1):
            h_copy(d, k).start()
    norm(1)
    load_w.wait()
    w_copy.wait_recv()
    lhs = lhs_of(0)

    def longer(b):
        return b[1] == 0

    def first(b, absorbed):
        project(0, b, lhs)
        for upward in (True, False):
            if not (absorbed and upward == longer(b)):
                chain(b, upward, 0).start()

    each(functools.partial(first, absorbed=True), 0, ABSORB)
    each(functools.partial(first, absorbed=False), ABSORB)
    hand_on()
    rest = lhs_of(1)
    await_all(head, h_recv)
    heads = [jnp.concatenate([head[d, 0], head[d, 1]], axis=1) for d in (0, 1)]

    await_all(wnext.at[:, pl.ds(kdim, kdim)], f_recv)
    for p in range(ABSORB):
        for d in (0, 1):
            b, upward = (p, d), d == 0
            theirs = dot(heads[d], wnext[d, :, p * block : (p + 1) * block])
            own = part[index(b), owed(b, upward, 1)].astype(F32)
            rbuf[index(b), slot(b, upward, 0)] = (theirs + own).astype(BF16)
            chain(b, upward, 1).start()
    each(lambda b: project(1, b, rest))

    def pass_on(b, hop, absorbed):
        for upward in (True, False):
            if hop < hops(b, upward) and not (absorbed and hop == 1 and upward == longer(b)):
                chain(b, upward, hop - 1).wait_recv()
                at = slot(b, upward, hop - 1)
                own = part[index(b), owed(b, upward, hop)].astype(F32)
                rbuf[index(b), at] = (rbuf[index(b), at].astype(F32) + own).astype(BF16)
                chain(b, upward, hop).start()

    for hop in range(1, far):
        each(functools.partial(pass_on, hop=hop, absorbed=True), 0, ABSORB)
        each(functools.partial(pass_on, hop=hop, absorbed=False), ABSORB)

    load_res.wait()

    def finish(b):
        at = pl.ds(column(b), wide)
        summed = resbuf[:, at].astype(F32) + part[index(b), place[0]].astype(F32)
        for upward in (True, False):
            last = hops(b, upward) - 1
            chain(b, upward, last).wait_recv()
            summed += rbuf[index(b), slot(b, upward, last)].astype(F32)
        out_ref[:, at] = summed.astype(BF16)

    each(finish)

    await_all(sbuf.at[pl.ds(0, NZ - 1)], a_send)
    await_all(psend.at[pl.ds(0, NZ - 1)], p_send)
    await_all(xbuf.at[pl.ds(0, nx - 1)], x_send)
    lax.fori_loop(0, nx - 1 - x, count(lambda d: await_all(direct.at[pl.ds(0, EARLY)], r_send.at[d])), 0)
    w_copy.wait_send()
    await_all(nrecv, core_send.at[1])
    await_all(wnext.at[:, pl.ds(0, kdim)], y_send)
    await_all(wnext.at[:, pl.ds(0, kdim)], f_send)
    await_all(head, h_send)
    sent = STREAMS * (ny - 1) - 2 * ABSORB
    await_all(wbuf.at[pl.ds(0, sent * mine // STREAMS)], ring_send)


def solution(mesh):
    nx, ny = mesh.shape["ctx"] // NZ, mesh.shape["exp"] // 2

    def shards(q_spikes, k_spikes, v_spikes, log_decay, norm_gain, out_weight, residual):
        rows = q_spikes.shape[0]
        kdim, width = out_weight.shape
        mine = residual.shape[0]
        wide = width // STREAMS
        vmem = pl.BlockSpec(memory_space=pltpu.VMEM)
        hbm = pl.BlockSpec(memory_space=pltpu.HBM)
        dma = pltpu.SemaphoreType.DMA
        args = (q_spikes, k_spikes, v_spikes, log_decay.T, norm_gain.reshape(1, -1), out_weight, residual)
        return pl.pallas_call(
            functools.partial(kernel, nx, ny),
            out_shape=pltpu.VMEM(residual.shape, BF16),
            in_specs=[hbm] * 7,
            out_specs=vmem,
            scratch_shapes=[
                pltpu.VMEM(q_spikes.shape, BF16),
                pltpu.VMEM((2, *q_spikes.shape), BF16),
                pltpu.VMEM((HEADS, rows), F32),
                pltpu.VMEM((1, kdim), F32),
                pltpu.VMEM((2 * kdim, width), BF16),
                pltpu.VMEM((mine, width), BF16),
                pltpu.VMEM((NZ, MSG, HD), BF16),
                pltpu.VMEM((NZ, MSG, HD), BF16),
                pltpu.VMEM((MSG, HD), BF16),
                pltpu.VMEM((nx, MSG, HD), BF16),
                pltpu.VMEM((NZ, BODY, HD), BF16),
                pltpu.VMEM((NZ, BODY, HD), BF16),
                pltpu.VMEM(((nx - 1) * NZ, BODY, HD), BF16),
                pltpu.VMEM((NZ, BODY, HD), F32),
                pltpu.VMEM((rows, HEADS * HD), F32),
                pltpu.VMEM((rows, HD), F32),
                pltpu.VMEM((ny, 2, mine, kdim), BF16),
                pltpu.VMEM((ny, mine, kdim), BF16),
                pltpu.VMEM((2, 2 * kdim, ABSORB * wide), BF16),
                pltpu.VMEM((2, 2, mine, kdim), BF16),
                pltpu.VMEM((STREAMS, ny, mine, wide), BF16),
                pltpu.VMEM((STREAMS, ny - 1, mine, wide), BF16),
                dma((6,)), dma((2,)), dma((3,)), dma, dma, dma, dma, dma, dma, dma((nx - 1,)), dma((nx - 1,)),
                dma, dma, dma, dma, dma, dma, dma, dma((STREAMS, ny - 1)),
            ],
            compiler_params=pltpu.CompilerParams(
                collective_id=0, has_side_effects=True, vmem_limit_bytes=48 * 2**20
            ),
        )(*[pltpu.with_memory_space_constraint(a, pltpu.HBM) for a in args])

    return jax.shard_map(
        shards,
        mesh=mesh,
        in_specs=(
            P("ctx", "exp"),
            P("ctx", "exp"),
            P("ctx", "exp"),
            P("ctx", "exp"),
            P("exp"),
            P("exp", None),
            P(("ctx", "exp"), None),
        ),
        out_specs=P(("ctx", "exp"), None),
        check_vma=False,
    )
```

```python
import functools

import jax
import jax.numpy as jnp
from jax import lax
from jax.experimental import pallas as pl
from jax.experimental.pallas import tpu as pltpu
from jax.sharding import PartitionSpec as P

MESH = pl.DeviceIdType.MESH
F32, BF16 = jnp.float32, jnp.bfloat16
NZ = 8
HEADS, HD = 2, 128
SLICE = HD // NZ
BODY = HEADS * SLICE
MSG = BODY + 16
EARLY = 2
STREAMS = 4
ABSORB = 1
NT = (((1,), (1,)), ((), ()))
TN = (((0,), (0,)), ((), ()))


def dot(a, b, dims=(((1,), (0,)), ((), ()))):
    return lax.dot_general(a, b, dims, preferred_element_type=F32)


def thirds(x):
    hi = x.astype(BF16).astype(F32)
    mid = (x - hi).astype(BF16).astype(F32)
    return hi, mid, x - hi - mid


def decay_tile(totals):
    row = lax.broadcasted_iota(jnp.int32, (16, HD), 0)
    tile = jnp.zeros((16, HD), F32)
    for h, total in enumerate(totals):
        for j, part in enumerate(thirds(total)):
            tile = jnp.where(row == 3 * h + j, part, tile)
    return tile.astype(BF16)


def read_decay(tile):
    t = tile.astype(F32)
    return [t[3 * h : 3 * h + 1] + t[3 * h + 1 : 3 * h + 2] + t[3 * h + 2 : 3 * h + 3] for h in range(HEADS)]


def per_head(pair):
    row = lax.broadcasted_iota(jnp.int32, (BODY, HD), 0)
    return jnp.where(row < SLICE, pair[0], pair[1])


def kernel(
    nx, ny,
    q_in, k_in, v_in, ld_in, gain_in, w_ref, res_ref, out_ref,
    q_ref, kv_ref, ld_ref, gain_ref, wbuf, resbuf, sbuf, abuf, xsend, xbuf, psend, pbuf, direct, entering, att, grown, nbuf, nrecv, wnext, head, part, rbuf,
    load_sem, core_send, core_recv, a_send, a_recv, x_send, x_recv, p_send, p_recv, r_send, r_recv, y_send, y_recv, f_send, f_recv, h_send, h_recv, ring_send, ring_recv,
):
    ctx, ex = lax.axis_index("ctx"), lax.axis_index("exp")
    x, z = ctx // NZ, lax.rem(ctx, NZ)
    y, core = ex // 2, lax.rem(ex, 2)
    rows = q_in.shape[0]
    kdim = w_ref.shape[0]
    mate = (ctx, y * 2 + 1 - core)
    up = (ctx, lax.rem(y + 1, ny) * 2 + core)
    down = (ctx, lax.rem(y + ny - 1, ny) * 2 + core)

    aslant = [(ctx, lax.rem(y + d, ny) * 2 + 1 - core) for d in (1, ny - 1)]

    def await_all(like, sem):
        pltpu.make_async_copy(like, like, sem).wait()

    def z_peer(j):
        return lax.rem(z + j, NZ)

    def x_peer(j):
        return lax.rem(x + j, nx)

    barrier = pltpu.get_barrier_semaphore()
    peers = [(x * NZ + z_peer(j), ex) for j in sorted(range(1, NZ), key=lambda j: -min(j, NZ - j))]
    peers += [(x_peer(j) * NZ + z, ex) for j in range(1, nx)]
    peers += [up, down, mate, *aslant]
    for peer in peers:
        pl.semaphore_signal(barrier, inc=1, device_id=peer, device_id_type=MESH)

    early = z < EARLY

    def greet(c, carry):
        @pl.when(lax.rem(c, NZ) != z)
        def _():
            pl.semaphore_signal(barrier, inc=1, device_id=(c, ex), device_id_type=MESH)

        return carry

    @pl.when(early)
    def _():
        lax.fori_loop(0, x * NZ, greet, 0)

    directs = (nx - 1 - x) * EARLY
    greeted = (nx - 1 - x) * (EARLY - early.astype(jnp.int32))

    k_ref, v_ref = kv_ref.at[0], kv_ref.at[1]
    loads = [
        pltpu.make_async_copy(a, b, load_sem.at[i])
        for a, b, i in (
            (ld_in, ld_ref, 2), (k_in, k_ref, 3), (v_in, v_ref, 3), (q_in, q_ref, 4), (gain_in, gain_ref, 5)
        )
    ]
    for load in loads:
        load.start()
    load_w = pltpu.make_async_copy(w_ref, wbuf.at[pl.ds(0, kdim)], load_sem.at[0])
    load_w.start()
    load_res = pltpu.make_async_copy(res_ref, resbuf, load_sem.at[1])
    load_res.start()

    loads[0].wait()
    ld = jnp.concatenate([ld_ref[...]] * (8 // HEADS), axis=0)
    hi, mid, lo = thirds(ld)
    kind = lax.broadcasted_iota(jnp.int32, ld.shape, 0) // HEADS
    parts = jnp.where(kind == 0, hi, jnp.where(kind == 1, mid, jnp.where(kind == 2, lo, 0.0))).astype(BF16)
    ti = lax.broadcasted_iota(jnp.int32, (rows, rows), 0)
    si = lax.broadcasted_iota(jnp.int32, (rows, rows), 1)
    tri = jnp.where(si <= ti, 1.0, 0.0).astype(BF16)
    by_col = dot(tri, parts, NT)
    by_row = dot(parts, tri, NT)
    cum_col = [by_col[:, h : h + 1] + by_col[:, 2 + h : 3 + h] + by_col[:, 4 + h : 5 + h] for h in range(HEADS)]
    cum_row = [by_row[h : h + 1] + by_row[2 + h : 3 + h] + by_row[4 + h : 5 + h] for h in range(HEADS)]
    total = [jnp.broadcast_to(c[rows - 1 : rows], (1, HD)) for c in cum_col]
    for h in range(HEADS):
        grown[:, h : h + 1] = jnp.exp(cum_col[h])

    tile = decay_tile(total)
    await_all(kv_ref, load_sem.at[3])
    for h in range(HEADS):
        cols = slice(h * HD, (h + 1) * HD)
        keyed = (k_ref[:, cols].astype(F32) * jnp.exp(total[h] - cum_col[h])).astype(BF16)
        state = dot(keyed, v_ref[:, cols], TN)
        sbuf[:, h * SLICE : (h + 1) * SLICE, :] = state.astype(BF16).reshape(NZ, SLICE, HD)
    for j in range(NZ):
        sbuf[j, BODY:MSG, :] = tile

    pl.semaphore_wait(barrier, len(peers) + greeted)

    def a_copy(j):
        return pltpu.make_async_remote_copy(
            sbuf.at[z_peer(j)], abuf.at[z], a_send, a_recv,
            device_id=(x * NZ + z_peer(j), ex), device_id_type=MESH,
        )

    def x_copy(j):
        return pltpu.make_async_remote_copy(
            xsend, xbuf.at[x], x_send, x_recv,
            device_id=(x_peer(j) * NZ + z, ex), device_id_type=MESH,
        )

    def p_copy(to):
        return pltpu.make_async_remote_copy(
            psend.at[to], pbuf.at[z], p_send, p_recv,
            device_id=(x * NZ + to, ex), device_id_type=MESH,
        )

    def others(indices, body):
        for i in indices:
            pl.when(z != i)(functools.partial(body, i))

    def r_copy(t):
        to = (x + 1 + t // EARLY) * NZ + lax.rem(t, EARLY)
        return pltpu.make_async_remote_copy(
            xsend.at[pl.ds(0, BODY)], direct.at[ctx], r_send.at[t // EARLY], r_recv.at[x], device_id=(to, ex), device_id_type=MESH
        )

    def count(body):
        def step(i, carry):
            body(i)
            return carry

        return step

    for j in sorted(range(1, NZ), key=lambda j: -min(j, NZ - j)):
        a_copy(j).start()
    w_copy = pltpu.make_async_remote_copy(
        w_ref, wbuf.at[pl.ds(kdim, kdim)], core_send.at[0], core_recv.at[0], device_id=mate, device_id_type=MESH
    )
    w_copy.start()
    half_cols = w_ref.shape[1] // 2
    block = half_cols // (STREAMS // 2)

    def y_copy(d, p):
        there = wnext.at[d, pl.ds(0, kdim), pl.ds(p * block, block)]
        return pltpu.make_async_remote_copy(
            w_ref.at[:, pl.ds(d * half_cols + p * block, block)], there, y_send, y_recv,
            device_id=(up, down)[d], device_id_type=MESH,
        )

    def f_copy(d, p):
        cols = pl.ds(p * block, block)
        return pltpu.make_async_remote_copy(
            wnext.at[d, pl.ds(0, kdim), cols], wnext.at[d, pl.ds(kdim, kdim), cols], f_send, f_recv,
            device_id=mate, device_id_type=MESH,
        )

    def hand_on():
        await_all(wnext.at[:, pl.ds(0, kdim)], y_recv)
        for p in range(ABSORB):
            for d in (0, 1):
                f_copy(d, p).start()

    for p in range(ABSORB):
        for d in (0, 1):
            y_copy(d, p).start()
    abuf[z] = sbuf[z]

    def attend(h, i):
        cols = slice(h * HD, (h + 1) * HD)
        r0, end = i * HD, (i + 1) * HD
        scores = dot(q_ref[r0:end, cols], k_ref[:end, cols], NT)
        spread = cum_col[h][r0:end] - cum_row[h][:, :end]
        at = lax.broadcasted_iota(jnp.int32, (HD, end), 0) + r0
        seen = lax.broadcasted_iota(jnp.int32, (HD, end), 1) <= at
        weight = jnp.exp(jnp.where(seen, spread, -1e30))
        att[r0:end, cols] = dot((scores * weight).astype(BF16), v_ref[:end, cols])

    loads[3].wait()
    loads[4].wait()
    for i in range(rows // HD):
        attend(0, i)

    await_all(abuf.at[pl.ds(0, NZ - 1)], a_recv)
    state = jnp.zeros((BODY, HD), F32)
    run = [jnp.zeros((1, HD), F32)] * HEADS
    inner, passed, row_decay = [], [], []
    for j in range(NZ):
        inner.append(state)
        passed.append(run)
        own = read_decay(abuf[j, BODY:MSG, :])
        row_decay.append(own)
        state = state * jnp.exp(per_head(own)) + abuf[j, :BODY, :].astype(F32)
        run = [a + b for a, b in zip(run, own)]
    xsend[:BODY, :] = state.astype(BF16)
    xsend[BODY:, :] = decay_tile(run)
    for t in reversed(range((nx - 1) * EARLY)):
        pl.when(t < directs)(lambda t=t: r_copy(t).start())
    for j in range(EARLY):
        psend[j] = inner[j].astype(BF16)
    others(range(EARLY), lambda i: p_copy(i).start())
    for j in range(1, nx):
        x_copy(j).start()
    xbuf[x] = xsend[...]

    for i in range(rows // HD - 1):
        attend(1, i)

    await_all(xbuf.at[pl.ds(0, nx - 1)], x_recv)
    base = jnp.zeros((BODY, HD), F32)
    for j in range(nx - 1):
        own = read_decay(xbuf[j, BODY:MSG, :])
        later = base * jnp.exp(per_head(own)) + xbuf[j, :BODY, :].astype(F32)
        base = jnp.where(j < x, later, base)
    for j in range(EARLY, NZ):
        psend[j] = (inner[j] + base * jnp.exp(per_head(passed[j]))).astype(BF16)
    others(range(EARLY, NZ), lambda i: p_copy(i).start())
    pbuf[z] = psend[z]

    attend(1, rows // HD - 1)

    await_all(pbuf.at[pl.ds(0, NZ - 1)], p_recv)

    @pl.when(early)
    def _():
        since = per_head([sum(jnp.where(j < z, own[h], 0.0) for j, own in enumerate(row_decay)) for h in range(HEADS)])
        entering[...] = jnp.zeros_like(entering)

        def join(row):
            await_all(direct.at[pl.ds(row * NZ, NZ)], r_recv.at[row])
            own = jnp.exp(per_head(read_decay(xbuf[row, BODY:MSG, :])))
            for j in range(NZ):
                entering[j] = entering[j] * own + direct[row * NZ + j].astype(F32)

        lax.fori_loop(0, x, count(join), 0)
        factor = jnp.exp(since)
        for j in range(NZ):
            pbuf[j] = (pbuf[j].astype(F32) + entering[j] * factor).astype(BF16)

    far = ny // 2
    order = [far, far - 1, 1 - far]
    for r in range(far - 2, 0, -1):
        order += [r, -r]
    order.append(0)
    place = {r % ny: i for i, r in enumerate(order)}
    near = rows // ny
    mine = near // 2
    wide = part.shape[-1]
    state_in = [pbuf[:, h * SLICE : (h + 1) * SLICE, :].reshape(HD, HD) for h in range(HEADS)]

    def n_copy(g):
        p = pl.ds(groups[g][0], groups[g][1])
        return pltpu.make_async_remote_copy(
            nbuf.at[p, 1 - core], nrecv.at[p], core_send.at[1], core_recv.at[1 + g],
            device_id=mate, device_id_type=MESH,
        )

    def norm(g):
        start, count = groups[g]
        at = [pl.ds(pl.multiple_of(lax.rem(y + r + ny, ny) * near, near), near) for r in order[start : start + count]]
        up_to = jnp.concatenate([grown[a] for a in at], axis=0)
        for h in range(HEADS):
            cols = slice(h * HD, (h + 1) * HD)
            query = jnp.concatenate([q_ref[a, cols] for a in at], axis=0)
            local = jnp.concatenate([att[a, cols] for a in at], axis=0)
            whole = local + dot(query, state_in[h]) * up_to[:, h : h + 1]
            mean = jnp.mean(whole * whole, axis=-1, keepdims=True)
            normed = whole * lax.rsqrt(mean + 1e-6) * gain_ref[:, cols]
            nbuf[start : start + count, :, :, cols] = normed.astype(BF16).reshape(count, 2, mine, HD)
        n_copy(g).start()

    def h_copy(d, k):
        return pltpu.make_async_remote_copy(
            nbuf.at[0, lax.rem(core + k, 2)], head.at[d, k], h_send, h_recv,
            device_id=(up, down)[d] if k == 0 else aslant[d], device_id_type=MESH,
        )

    def project(g, b, lhs):
        start, count = groups[g]
        c0 = column(b)
        part[index(b), start : start + count] = dot(lhs, wbuf[:, pl.ds(c0, wide)]).astype(BF16).reshape(count, mine, wide)

    def lhs_of(g):
        start, count = groups[g]
        n_copy(g).wait_recv()
        own = nbuf[start : start + count, core].reshape(count * mine, kdim)
        other = nrecv[start : start + count].reshape(count * mine, kdim)
        return jnp.concatenate([own, other], axis=1)

    def column(b):
        pair, half = b
        c0 = half * (STREAMS // 2) * wide
        return c0 + pair * wide if isinstance(pair, int) else pl.multiple_of(c0 + pair * wide, wide)

    def index(b):
        return b[0] * 2 + b[1]

    def hops(b, upward):
        return far if (b[1] == 0) == upward else far - 1

    def owed(b, upward, hop):
        left = hops(b, upward) - hop
        return place[(left if upward else -left) % ny]

    def slot(b, upward, hop):
        return hop if upward else hops(b, True) + hop

    def chain(b, upward, hop):
        source = part.at[index(b), owed(b, upward, hop)] if hop == 0 else rbuf.at[index(b), slot(b, upward, hop - 1)]
        at = slot(b, upward, hop)
        return pltpu.make_async_remote_copy(
            source, rbuf.at[index(b), at], ring_send, ring_recv.at[index(b), at],
            device_id=up if upward else down, device_id_type=MESH,
        )

    def each(body, start=0, end=STREAMS // 2):
        def step(pair, carry):
            for half in (0, 1):
                body((pair, half))
            return carry

        lax.fori_loop(start, end, step, 0)

    groups = [(0, 3), (3, ny - 3)]
    norm(0)
    for d in (0, 1):
        for k in (0, 1):
            h_copy(d, k).start()
    norm(1)
    load_w.wait()
    w_copy.wait_recv()
    lhs = lhs_of(0)

    def longer(b):
        return b[1] == 0

    def first(b, absorbed):
        project(0, b, lhs)
        for upward in (True, False):
            if not (absorbed and upward == longer(b)):
                chain(b, upward, 0).start()

    each(functools.partial(first, absorbed=True), 0, ABSORB)
    each(functools.partial(first, absorbed=False), ABSORB)
    hand_on()
    rest = lhs_of(1)
    await_all(head, h_recv)
    heads = [jnp.concatenate([head[d, 0], head[d, 1]], axis=1) for d in (0, 1)]

    await_all(wnext.at[:, pl.ds(kdim, kdim)], f_recv)
    for p in range(ABSORB):
        for d in (0, 1):
            b, upward = (p, d), d == 0
            theirs = dot(heads[d], wnext[d, :, p * block : (p + 1) * block])
            own = part[index(b), owed(b, upward, 1)].astype(F32)
            rbuf[index(b), slot(b, upward, 0)] = (theirs + own).astype(BF16)
            chain(b, upward, 1).start()
    each(lambda b: project(1, b, rest))

    def pass_on(b, hop, absorbed):
        for upward in (True, False):
            if hop < hops(b, upward) and not (absorbed and hop == 1 and upward == longer(b)):
                chain(b, upward, hop - 1).wait_recv()
                at = slot(b, upward, hop - 1)
                own = part[index(b), owed(b, upward, hop)].astype(F32)
                rbuf[index(b), at] = (rbuf[index(b), at].astype(F32) + own).astype(BF16)
                chain(b, upward, hop).start()

    for hop in range(1, far):
        each(functools.partial(pass_on, hop=hop, absorbed=True), 0, ABSORB)
        each(functools.partial(pass_on, hop=hop, absorbed=False), ABSORB)

    load_res.wait()

    def finish(b):
        at = pl.ds(column(b), wide)
        summed = resbuf[:, at].astype(F32) + part[index(b), place[0]].astype(F32)
        for upward in (True, False):
            last = hops(b, upward) - 1
            chain(b, upward, last).wait_recv()
            summed += rbuf[index(b), slot(b, upward, last)].astype(F32)
        out_ref[:, at] = summed.astype(BF16)

    each(finish)

    await_all(sbuf.at[pl.ds(0, NZ - 1)], a_send)
    await_all(psend.at[pl.ds(0, NZ - 1)], p_send)
    await_all(xbuf.at[pl.ds(0, nx - 1)], x_send)
    lax.fori_loop(0, nx - 1 - x, count(lambda d: await_all(direct.at[pl.ds(0, EARLY)], r_send.at[d])), 0)
    w_copy.wait_send()
    await_all(nrecv, core_send.at[1])
    await_all(wnext.at[:, pl.ds(0, kdim)], y_send)
    await_all(wnext.at[:, pl.ds(0, kdim)], f_send)
    await_all(head, h_send)
    sent = STREAMS * (ny - 1) - 2 * ABSORB
    await_all(wbuf.at[pl.ds(0, sent * mine // STREAMS)], ring_send)


def solution(mesh):
    nx, ny = mesh.shape["ctx"] // NZ, mesh.shape["exp"] // 2

    def shards(q_spikes, k_spikes, v_spikes, log_decay, norm_gain, out_weight, residual):
        rows = q_spikes.shape[0]
        kdim, width = out_weight.shape
        mine = residual.shape[0]
        wide = width // STREAMS
        vmem = pl.BlockSpec(memory_space=pltpu.VMEM)
        hbm = pl.BlockSpec(memory_space=pltpu.HBM)
        dma = pltpu.SemaphoreType.DMA
        args = (q_spikes, k_spikes, v_spikes, log_decay.T, norm_gain.reshape(1, -1), out_weight, residual)
        return pl.pallas_call(
            functools.partial(kernel, nx, ny),
            out_shape=pltpu.VMEM(residual.shape, BF16),
            in_specs=[hbm] * 7,
            out_specs=vmem,
            scratch_shapes=[
                pltpu.VMEM(q_spikes.shape, BF16),
                pltpu.VMEM((2, *q_spikes.shape), BF16),
                pltpu.VMEM((HEADS, rows), F32),
                pltpu.VMEM((1, kdim), F32),
                pltpu.VMEM((2 * kdim, width), BF16),
                pltpu.VMEM((mine, width), BF16),
                pltpu.VMEM((NZ, MSG, HD), BF16),
                pltpu.VMEM((NZ, MSG, HD), BF16),
                pltpu.VMEM((MSG, HD), BF16),
                pltpu.VMEM((nx, MSG, HD), BF16),
                pltpu.VMEM((NZ, BODY, HD), BF16),
                pltpu.VMEM((NZ, BODY, HD), BF16),
                pltpu.VMEM(((nx - 1) * NZ, BODY, HD), BF16),
                pltpu.VMEM((NZ, BODY, HD), F32),
                pltpu.VMEM((rows, HEADS * HD), F32),
                pltpu.VMEM((rows, HD), F32),
                pltpu.VMEM((ny, 2, mine, kdim), BF16),
                pltpu.VMEM((ny, mine, kdim), BF16),
                pltpu.VMEM((2, 2 * kdim, ABSORB * wide), BF16),
                pltpu.VMEM((2, 2, mine, kdim), BF16),
                pltpu.VMEM((STREAMS, ny, mine, wide), BF16),
                pltpu.VMEM((STREAMS, ny - 1, mine, wide), BF16),
                dma((6,)), dma((2,)), dma((3,)), dma, dma, dma, dma, dma, dma, dma((nx - 1,)), dma((nx - 1,)),
                dma, dma, dma, dma, dma, dma, dma, dma((STREAMS, ny - 1)),
            ],
            compiler_params=pltpu.CompilerParams(
                collective_id=0, has_side_effects=True, vmem_limit_bytes=48 * 2**20
            ),
        )(*[pltpu.with_memory_space_constraint(a, pltpu.HBM) for a in args])

    return jax.shard_map(
        shards,
        mesh=mesh,
        in_specs=(
            P("ctx", "exp"),
            P("ctx", "exp"),
            P("ctx", "exp"),
            P("ctx", "exp"),
            P("exp"),
            P("exp", None),
            P(("ctx", "exp"), None),
        ),
        out_specs=P(("ctx", "exp"), None),
        check_vma=False,
    )
```

```python
import functools

import jax
import jax.numpy as jnp
from jax import lax
from jax.experimental import pallas as pl
from jax.experimental.pallas import tpu as pltpu
from jax.sharding import PartitionSpec as P

MESH = pl.DeviceIdType.MESH
F32, BF16 = jnp.float32, jnp.bfloat16
NZ = 8
HEADS, HD = 2, 128
SLICE = HD // NZ
BODY = HEADS * SLICE
MSG = BODY + 16
EARLY = 2
STREAMS = 4
ABSORB = 1
NT = (((1,), (1,)), ((), ()))
TN = (((0,), (0,)), ((), ()))


def dot(a, b, dims=(((1,), (0,)), ((), ()))):
    return lax.dot_general(a, b, dims, preferred_element_type=F32)


def thirds(x):
    hi = x.astype(BF16).astype(F32)
    mid = (x - hi).astype(BF16).astype(F32)
    return hi, mid, x - hi - mid


def decay_tile(totals):
    row = lax.broadcasted_iota(jnp.int32, (16, HD), 0)
    tile = jnp.zeros((16, HD), F32)
    for h, total in enumerate(totals):
        for j, part in enumerate(thirds(total)):
            tile = jnp.where(row == 3 * h + j, part, tile)
    return tile.astype(BF16)


def read_decay(tile):
    t = tile.astype(F32)
    return [t[3 * h : 3 * h + 1] + t[3 * h + 1 : 3 * h + 2] + t[3 * h + 2 : 3 * h + 3] for h in range(HEADS)]


def per_head(pair):
    row = lax.broadcasted_iota(jnp.int32, (BODY, HD), 0)
    return jnp.where(row < SLICE, pair[0], pair[1])


def kernel(
    nx, ny,
    q_in, k_in, v_in, ld_in, gain_in, w_ref, res_ref, out_ref,
    q_ref, kv_ref, ld_ref, gain_ref, wbuf, resbuf, sbuf, abuf, xsend, xbuf, psend, pbuf, direct, entering, att, grown, nbuf, nrecv, wnext, head, part, rbuf,
    load_sem, core_send, core_recv, a_send, a_recv, x_send, x_recv, p_send, p_recv, r_send, r_recv, y_send, y_recv, f_send, f_recv, h_send, h_recv, ring_send, ring_recv,
):
    ctx, ex = lax.axis_index("ctx"), lax.axis_index("exp")
    x, z = ctx // NZ, lax.rem(ctx, NZ)
    y, core = ex // 2, lax.rem(ex, 2)
    rows = q_in.shape[0]
    kdim = w_ref.shape[0]
    mate = (ctx, y * 2 + 1 - core)
    up = (ctx, lax.rem(y + 1, ny) * 2 + core)
    down = (ctx, lax.rem(y + ny - 1, ny) * 2 + core)

    aslant = [(ctx, lax.rem(y + d, ny) * 2 + 1 - core) for d in (1, ny - 1)]

    def await_all(like, sem):
        pltpu.make_async_copy(like, like, sem).wait()

    def z_peer(j):
        return lax.rem(z + j, NZ)

    def x_peer(j):
        return lax.rem(x + j, nx)

    barrier = pltpu.get_barrier_semaphore()
    peers = [(x * NZ + z_peer(j), ex) for j in sorted(range(1, NZ), key=lambda j: -min(j, NZ - j))]
    peers += [(x_peer(j) * NZ + z, ex) for j in range(1, nx)]
    peers += [up, down, mate, *aslant]
    for peer in peers:
        pl.semaphore_signal(barrier, inc=1, device_id=peer, device_id_type=MESH)

    early = z < EARLY

    def greet(c, carry):
        @pl.when(lax.rem(c, NZ) != z)
        def _():
            pl.semaphore_signal(barrier, inc=1, device_id=(c, ex), device_id_type=MESH)

        return carry

    @pl.when(early)
    def _():
        lax.fori_loop(0, x * NZ, greet, 0)

    directs = (nx - 1 - x) * EARLY
    greeted = (nx - 1 - x) * (EARLY - early.astype(jnp.int32))

    k_ref, v_ref = kv_ref.at[0], kv_ref.at[1]
    loads = [
        pltpu.make_async_copy(a, b, load_sem.at[i])
        for a, b, i in (
            (ld_in, ld_ref, 2), (k_in, k_ref, 3), (v_in, v_ref, 3), (q_in, q_ref, 4), (gain_in, gain_ref, 5)
        )
    ]
    for load in loads:
        load.start()
    load_w = pltpu.make_async_copy(w_ref, wbuf.at[pl.ds(0, kdim)], load_sem.at[0])
    load_w.start()
    load_res = pltpu.make_async_copy(res_ref, resbuf, load_sem.at[1])
    load_res.start()

    loads[0].wait()
    ld = jnp.concatenate([ld_ref[...]] * (8 // HEADS), axis=0)
    hi, mid, lo = thirds(ld)
    kind = lax.broadcasted_iota(jnp.int32, ld.shape, 0) // HEADS
    parts = jnp.where(kind == 0, hi, jnp.where(kind == 1, mid, jnp.where(kind == 2, lo, 0.0))).astype(BF16)
    ti = lax.broadcasted_iota(jnp.int32, (rows, rows), 0)
    si = lax.broadcasted_iota(jnp.int32, (rows, rows), 1)
    tri = jnp.where(si <= ti, 1.0, 0.0).astype(BF16)
    by_col = dot(tri, parts, NT)
    by_row = dot(parts, tri, NT)
    cum_col = [by_col[:, h : h + 1] + by_col[:, 2 + h : 3 + h] + by_col[:, 4 + h : 5 + h] for h in range(HEADS)]
    cum_row = [by_row[h : h + 1] + by_row[2 + h : 3 + h] + by_row[4 + h : 5 + h] for h in range(HEADS)]
    total = [jnp.broadcast_to(c[rows - 1 : rows], (1, HD)) for c in cum_col]
    for h in range(HEADS):
        grown[:, h : h + 1] = jnp.exp(cum_col[h])

    tile = decay_tile(total)
    await_all(kv_ref, load_sem.at[3])
    for h in range(HEADS):
        cols = slice(h * HD, (h + 1) * HD)
        keyed = (k_ref[:, cols].astype(F32) * jnp.exp(total[h] - cum_col[h])).astype(BF16)
        state = dot(keyed, v_ref[:, cols], TN)
        sbuf[:, h * SLICE : (h + 1) * SLICE, :] = state.astype(BF16).reshape(NZ, SLICE, HD)
    for j in range(NZ):
        sbuf[j, BODY:MSG, :] = tile

    pl.semaphore_wait(barrier, len(peers) + greeted)

    def a_copy(j):
        return pltpu.make_async_remote_copy(
            sbuf.at[z_peer(j)], abuf.at[z], a_send, a_recv,
            device_id=(x * NZ + z_peer(j), ex), device_id_type=MESH,
        )

    def x_copy(j):
        return pltpu.make_async_remote_copy(
            xsend, xbuf.at[x], x_send, x_recv,
            device_id=(x_peer(j) * NZ + z, ex), device_id_type=MESH,
        )

    def p_copy(to):
        return pltpu.make_async_remote_copy(
            psend.at[to], pbuf.at[z], p_send, p_recv,
            device_id=(x * NZ + to, ex), device_id_type=MESH,
        )

    def others(indices, body):
        for i in indices:
            pl.when(z != i)(functools.partial(body, i))

    def r_copy(t):
        to = (x + 1 + t // EARLY) * NZ + lax.rem(t, EARLY)
        return pltpu.make_async_remote_copy(
            xsend.at[pl.ds(0, BODY)], direct.at[ctx], r_send.at[t // EARLY], r_recv.at[x], device_id=(to, ex), device_id_type=MESH
        )

    def count(body):
        def step(i, carry):
            body(i)
            return carry

        return step

    for j in sorted(range(1, NZ), key=lambda j: -min(j, NZ - j)):
        a_copy(j).start()
    w_copy = pltpu.make_async_remote_copy(
        w_ref, wbuf.at[pl.ds(kdim, kdim)], core_send.at[0], core_recv.at[0], device_id=mate, device_id_type=MESH
    )
    w_copy.start()
    half_cols = w_ref.shape[1] // 2
    block = half_cols // (STREAMS // 2)

    def y_copy(d, p):
        there = wnext.at[d, pl.ds(0, kdim), pl.ds(p * block, block)]
        return pltpu.make_async_remote_copy(
            w_ref.at[:, pl.ds(d * half_cols + p * block, block)], there, y_send, y_recv,
            device_id=(up, down)[d], device_id_type=MESH,
        )

    def f_copy(d, p):
        cols = pl.ds(p * block, block)
        return pltpu.make_async_remote_copy(
            wnext.at[d, pl.ds(0, kdim), cols], wnext.at[d, pl.ds(kdim, kdim), cols], f_send, f_recv,
            device_id=mate, device_id_type=MESH,
        )

    def hand_on():
        await_all(wnext.at[:, pl.ds(0, kdim)], y_recv)
        for p in range(ABSORB):
            for d in (0, 1):
                f_copy(d, p).start()

    for p in range(ABSORB):
        for d in (0, 1):
            y_copy(d, p).start()
    abuf[z] = sbuf[z]

    def attend(h, i):
        cols = slice(h * HD, (h + 1) * HD)
        r0, end = i * HD, (i + 1) * HD
        scores = dot(q_ref[r0:end, cols], k_ref[:end, cols], NT)
        spread = cum_col[h][r0:end] - cum_row[h][:, :end]
        at = lax.broadcasted_iota(jnp.int32, (HD, end), 0) + r0
        seen = lax.broadcasted_iota(jnp.int32, (HD, end), 1) <= at
        weight = jnp.exp(jnp.where(seen, spread, -1e30))
        att[r0:end, cols] = dot((scores * weight).astype(BF16), v_ref[:end, cols])

    loads[3].wait()
    loads[4].wait()
    for i in range(rows // HD):
        attend(0, i)

    await_all(abuf.at[pl.ds(0, NZ - 1)], a_recv)
    state = jnp.zeros((BODY, HD), F32)
    run = [jnp.zeros((1, HD), F32)] * HEADS
    inner, passed, row_decay = [], [], []
    for j in range(NZ):
        inner.append(state)
        passed.append(run)
        own = read_decay(abuf[j, BODY:MSG, :])
        row_decay.append(own)
        state = state * jnp.exp(per_head(own)) + abuf[j, :BODY, :].astype(F32)
        run = [a + b for a, b in zip(run, own)]
    xsend[:BODY, :] = state.astype(BF16)
    xsend[BODY:, :] = decay_tile(run)
    for t in reversed(range((nx - 1) * EARLY)):
        pl.when(t < directs)(lambda t=t: r_copy(t).start())
    for j in range(EARLY):
        psend[j] = inner[j].astype(BF16)
    others(range(EARLY), lambda i: p_copy(i).start())
    for j in sorted(range(1, nx), key=lambda j: -min(j, nx - j)):
        x_copy(j).start()
    xbuf[x] = xsend[...]

    for i in range(rows // HD - 1):
        attend(1, i)

    await_all(xbuf.at[pl.ds(0, nx - 1)], x_recv)
    base = jnp.zeros((BODY, HD), F32)
    for j in range(nx - 1):
        own = read_decay(xbuf[j, BODY:MSG, :])
        later = base * jnp.exp(per_head(own)) + xbuf[j, :BODY, :].astype(F32)
        base = jnp.where(j < x, later, base)
    for j in range(EARLY, NZ):
        psend[j] = (inner[j] + base * jnp.exp(per_head(passed[j]))).astype(BF16)
    for j in sorted(range(1, NZ), key=lambda j: -min(j, NZ - j)):
        pl.when(z_peer(j) >= EARLY)(lambda j=j: p_copy(z_peer(j)).start())
    pbuf[z] = psend[z]

    attend(1, rows // HD - 1)

    await_all(pbuf.at[pl.ds(0, NZ - 1)], p_recv)

    @pl.when(early)
    def _():
        since = per_head([sum(jnp.where(j < z, own[h], 0.0) for j, own in enumerate(row_decay)) for h in range(HEADS)])
        entering[...] = jnp.zeros_like(entering)

        def join(row):
            await_all(direct.at[pl.ds(row * NZ, NZ)], r_recv.at[row])
            own = jnp.exp(per_head(read_decay(xbuf[row, BODY:MSG, :])))
            for j in range(NZ):
                entering[j] = entering[j] * own + direct[row * NZ + j].astype(F32)

        lax.fori_loop(0, x, count(join), 0)
        factor = jnp.exp(since)
        for j in range(NZ):
            pbuf[j] = (pbuf[j].astype(F32) + entering[j] * factor).astype(BF16)

    far = ny // 2
    order = [far, far - 1, 1 - far]
    for r in range(far - 2, 0, -1):
        order += [r, -r]
    order.append(0)
    place = {r % ny: i for i, r in enumerate(order)}
    near = rows // ny
    mine = near // 2
    wide = part.shape[-1]
    state_in = [pbuf[:, h * SLICE : (h + 1) * SLICE, :].reshape(HD, HD) for h in range(HEADS)]

    def n_copy(g):
        p = pl.ds(groups[g][0], groups[g][1])
        return pltpu.make_async_remote_copy(
            nbuf.at[p, 1 - core], nrecv.at[p], core_send.at[1], core_recv.at[1 + g],
            device_id=mate, device_id_type=MESH,
        )

    def norm(g):
        start, count = groups[g]
        at = [pl.ds(pl.multiple_of(lax.rem(y + r + ny, ny) * near, near), near) for r in order[start : start + count]]
        up_to = jnp.concatenate([grown[a] for a in at], axis=0)
        for h in range(HEADS):
            cols = slice(h * HD, (h + 1) * HD)
            query = jnp.concatenate([q_ref[a, cols] for a in at], axis=0)
            local = jnp.concatenate([att[a, cols] for a in at], axis=0)
            whole = local + dot(query, state_in[h]) * up_to[:, h : h + 1]
            mean = jnp.mean(whole * whole, axis=-1, keepdims=True)
            normed = whole * lax.rsqrt(mean + 1e-6) * gain_ref[:, cols]
            nbuf[start : start + count, :, :, cols] = normed.astype(BF16).reshape(count, 2, mine, HD)
        n_copy(g).start()

    def h_copy(d, k):
        return pltpu.make_async_remote_copy(
            nbuf.at[0, lax.rem(core + k, 2)], head.at[d, k], h_send, h_recv,
            device_id=(up, down)[d] if k == 0 else aslant[d], device_id_type=MESH,
        )

    def project(g, b, lhs):
        start, count = groups[g]
        c0 = column(b)
        part[index(b), start : start + count] = dot(lhs, wbuf[:, pl.ds(c0, wide)]).astype(BF16).reshape(count, mine, wide)

    def lhs_of(g):
        start, count = groups[g]
        n_copy(g).wait_recv()
        own = nbuf[start : start + count, core].reshape(count * mine, kdim)
        other = nrecv[start : start + count].reshape(count * mine, kdim)
        return jnp.concatenate([own, other], axis=1)

    def column(b):
        pair, half = b
        c0 = half * (STREAMS // 2) * wide
        return c0 + pair * wide if isinstance(pair, int) else pl.multiple_of(c0 + pair * wide, wide)

    def index(b):
        return b[0] * 2 + b[1]

    def hops(b, upward):
        return far if (b[1] == 0) == upward else far - 1

    def owed(b, upward, hop):
        left = hops(b, upward) - hop
        return place[(left if upward else -left) % ny]

    def slot(b, upward, hop):
        return hop if upward else hops(b, True) + hop

    def chain(b, upward, hop):
        source = part.at[index(b), owed(b, upward, hop)] if hop == 0 else rbuf.at[index(b), slot(b, upward, hop - 1)]
        at = slot(b, upward, hop)
        return pltpu.make_async_remote_copy(
            source, rbuf.at[index(b), at], ring_send, ring_recv.at[index(b), at],
            device_id=up if upward else down, device_id_type=MESH,
        )

    def each(body, start=0, end=STREAMS // 2):
        def step(pair, carry):
            for half in (0, 1):
                body((pair, half))
            return carry

        lax.fori_loop(start, end, step, 0)

    groups = [(0, 3), (3, ny - 3)]
    norm(0)
    for d in (0, 1):
        for k in (0, 1):
            h_copy(d, k).start()
    norm(1)
    load_w.wait()
    w_copy.wait_recv()
    lhs = lhs_of(0)

    def longer(b):
        return b[1] == 0

    def first(b, absorbed):
        project(0, b, lhs)
        for upward in (True, False):
            if not (absorbed and upward == longer(b)):
                chain(b, upward, 0).start()

    each(functools.partial(first, absorbed=True), 0, ABSORB)
    each(functools.partial(first, absorbed=False), ABSORB)
    hand_on()
    rest = lhs_of(1)
    await_all(head, h_recv)
    heads = [jnp.concatenate([head[d, 0], head[d, 1]], axis=1) for d in (0, 1)]

    await_all(wnext.at[:, pl.ds(kdim, kdim)], f_recv)
    for p in range(ABSORB):
        for d in (0, 1):
            b, upward = (p, d), d == 0
            theirs = dot(heads[d], wnext[d, :, p * block : (p + 1) * block])
            own = part[index(b), owed(b, upward, 1)].astype(F32)
            rbuf[index(b), slot(b, upward, 0)] = (theirs + own).astype(BF16)
            chain(b, upward, 1).start()
    each(lambda b: project(1, b, rest))

    def pass_on(b, hop, absorbed):
        for upward in (True, False):
            if hop < hops(b, upward) and not (absorbed and hop == 1 and upward == longer(b)):
                chain(b, upward, hop - 1).wait_recv()
                at = slot(b, upward, hop - 1)
                own = part[index(b), owed(b, upward, hop)].astype(F32)
                rbuf[index(b), at] = (rbuf[index(b), at].astype(F32) + own).astype(BF16)
                chain(b, upward, hop).start()

    for hop in range(1, far):
        each(functools.partial(pass_on, hop=hop, absorbed=True), 0, ABSORB)
        each(functools.partial(pass_on, hop=hop, absorbed=False), ABSORB)

    load_res.wait()

    def finish(b):
        at = pl.ds(column(b), wide)
        summed = resbuf[:, at].astype(F32) + part[index(b), place[0]].astype(F32)
        for upward in (True, False):
            last = hops(b, upward) - 1
            chain(b, upward, last).wait_recv()
            summed += rbuf[index(b), slot(b, upward, last)].astype(F32)
        out_ref[:, at] = summed.astype(BF16)

    each(finish)

    await_all(sbuf.at[pl.ds(0, NZ - 1)], a_send)
    await_all(psend.at[pl.ds(0, NZ - 1)], p_send)
    await_all(xbuf.at[pl.ds(0, nx - 1)], x_send)
    lax.fori_loop(0, nx - 1 - x, count(lambda d: await_all(direct.at[pl.ds(0, EARLY)], r_send.at[d])), 0)
    w_copy.wait_send()
    await_all(nrecv, core_send.at[1])
    await_all(wnext.at[:, pl.ds(0, kdim)], y_send)
    await_all(wnext.at[:, pl.ds(0, kdim)], f_send)
    await_all(head, h_send)
    sent = STREAMS * (ny - 1) - 2 * ABSORB
    await_all(wbuf.at[pl.ds(0, sent * mine // STREAMS)], ring_send)


def solution(mesh):
    nx, ny = mesh.shape["ctx"] // NZ, mesh.shape["exp"] // 2

    def shards(q_spikes, k_spikes, v_spikes, log_decay, norm_gain, out_weight, residual):
        rows = q_spikes.shape[0]
        kdim, width = out_weight.shape
        mine = residual.shape[0]
        wide = width // STREAMS
        vmem = pl.BlockSpec(memory_space=pltpu.VMEM)
        hbm = pl.BlockSpec(memory_space=pltpu.HBM)
        dma = pltpu.SemaphoreType.DMA
        args = (q_spikes, k_spikes, v_spikes, log_decay.T, norm_gain.reshape(1, -1), out_weight, residual)
        return pl.pallas_call(
            functools.partial(kernel, nx, ny),
            out_shape=pltpu.VMEM(residual.shape, BF16),
            in_specs=[hbm] * 7,
            out_specs=vmem,
            scratch_shapes=[
                pltpu.VMEM(q_spikes.shape, BF16),
                pltpu.VMEM((2, *q_spikes.shape), BF16),
                pltpu.VMEM((HEADS, rows), F32),
                pltpu.VMEM((1, kdim), F32),
                pltpu.VMEM((2 * kdim, width), BF16),
                pltpu.VMEM((mine, width), BF16),
                pltpu.VMEM((NZ, MSG, HD), BF16),
                pltpu.VMEM((NZ, MSG, HD), BF16),
                pltpu.VMEM((MSG, HD), BF16),
                pltpu.VMEM((nx, MSG, HD), BF16),
                pltpu.VMEM((NZ, BODY, HD), BF16),
                pltpu.VMEM((NZ, BODY, HD), BF16),
                pltpu.VMEM(((nx - 1) * NZ, BODY, HD), BF16),
                pltpu.VMEM((NZ, BODY, HD), F32),
                pltpu.VMEM((rows, HEADS * HD), F32),
                pltpu.VMEM((rows, HD), F32),
                pltpu.VMEM((ny, 2, mine, kdim), BF16),
                pltpu.VMEM((ny, mine, kdim), BF16),
                pltpu.VMEM((2, 2 * kdim, ABSORB * wide), BF16),
                pltpu.VMEM((2, 2, mine, kdim), BF16),
                pltpu.VMEM((STREAMS, ny, mine, wide), BF16),
                pltpu.VMEM((STREAMS, ny - 1, mine, wide), BF16),
                dma((6,)), dma((2,)), dma((3,)), dma, dma, dma, dma, dma, dma, dma((nx - 1,)), dma((nx - 1,)),
                dma, dma, dma, dma, dma, dma, dma, dma((STREAMS, ny - 1)),
            ],
            compiler_params=pltpu.CompilerParams(
                collective_id=0, has_side_effects=True, vmem_limit_bytes=48 * 2**20
            ),
        )(*[pltpu.with_memory_space_constraint(a, pltpu.HBM) for a in args])

    return jax.shard_map(
        shards,
        mesh=mesh,
        in_specs=(
            P("ctx", "exp"),
            P("ctx", "exp"),
            P("ctx", "exp"),
            P("ctx", "exp"),
            P("exp"),
            P("exp", None),
            P(("ctx", "exp"), None),
        ),
        out_specs=P(("ctx", "exp"), None),
        check_vma=False,
    )
```
